128 devices in a mesh: af: 16 (over y_hi, x, core), gz: 8 (over z, y_lo).
Axes of the slice: x: 4, y: 4 (y_hi: 2, y_lo: 2; y = y_hi * 2 + y_lo), z: 4, core: 2. Of those that a mesh axis runs over, the one named last changes fastest.
Arguments:
- inputs: bfloat16 [512, 32, 1024], P('af', 'gz'), may hold values from -6 to 6
- preact: bfloat16 [512, 32, 1024], P('af', 'gz'), may hold values from -6 to 6
- cotangent: bfloat16 [512, 32, 1024], P('af', 'gz'), may hold values from -6 to 6
- weight1: bfloat16 [3, 3, 3, 512, 512], P(None, None, None, 'af'), may hold values from -0.0546875 to 0.0546875
- weight2: bfloat16 [3, 3, 3, 512, 512], P(None, None, None, 'af'), may hold values from -0.0546875 to 0.0546875
Outputs:
- input_grad: bfloat16 [32, 32, 32, 512], P('gz', 'af')
- filter1_grad: float32 [3, 3, 3, 512, 512], P(None, None, None, ('af', 'gz'))
- filter2_grad: float32 [3, 3, 3, 512, 512], P(None, None, None, ('af', 'gz'))
The draws below stay inside these ranges and needn't reach their ends.
All inputs are finite; a program needn't handle non-finite values.
Results may differ from the reference program's by a relative error of at most 0.017.
Values may be sent and summed in bfloat16 or wider, within the bound.
No kernel may reach another device: no remote copies, remote signals or barrier semaphores. Data moves between devices by JAX's collectives and lax.ppermute only.
A program may use at most 256 MiB of HBM per device.

```python
import jax
import jax.numpy as jnp

C = 512
Y = 32
X = 32
NZ = 32


def shard_levels(rng, dims, cuts, smallest, high):
    factor_of, own = 1.0, jax.random.fold_in(rng, 6)
    for dim, shards_of in cuts:
        heights = jnp.exp(jax.random.uniform(jax.random.fold_in(own, dim), (shards_of,), jnp.float32, smallest / len(cuts), high / len(cuts)))
        factor_of = factor_of * jnp.repeat(heights, dims[dim] // shards_of).reshape([-1 if axis == dim else 1 for axis in range(len(dims))])
    return factor_of


def gaussian(key, dims, deviation, limit, shards=(), kind=jnp.bfloat16):
    loudness = shard_levels(key, dims, shards, -0.22, 0.18) if shards else 1.0
    array = jax.random.normal(key, dims, jnp.float32) * deviation * loudness
    return jnp.minimum(jnp.maximum(array, -limit), limit).astype(kind)


def setup_inputs(seed: int = 0) -> dict:
    keys = jax.random.split(jax.random.key(seed), 6)
    return {
        "inputs": gaussian(keys[0], (C, NZ, Y * X), 1.0, 6.0, ((0, 16), (1, 8))),
        "preact": gaussian(keys[1], (C, NZ, Y * X), 1.0, 6.0, ((0, 16), (1, 8))),
        "cotangent": gaussian(keys[2], (C, NZ, Y * X), 1.0, 6.0, ((0, 16), (1, 8))),
        "weight1": gaussian(keys[3], (3, 3, 3, C, C), (27 * C) ** -0.5, 0.0546875, ((3, 16),)),
        "weight2": gaussian(keys[4], (3, 3, 3, C, C), (27 * C) ** -0.5, 0.0546875, ((3, 16),)),
    }


def pad_space(volume):
    return jnp.pad(volume, ((0, 0), (1, 1), (1, 1), (1, 1)))

def filter_grad(source, gradient):
    chans, depth_n, height_n, width_n = source.shape
    padded = pad_space(source)
    flat_grad = gradient.reshape(gradient.shape[0], -1)
    pieces = []
    for depth in range(3):
        for height in range(3):
            for across in range(3):
                window = padded[:, depth:depth + depth_n, height:height + height_n, across:across + width_n].reshape(chans, -1)
                pieces.append(jnp.dot(flat_grad, window.T, preferred_element_type=jnp.float32))
    return jnp.stack(pieces).reshape(3, 3, 3, gradient.shape[0], chans)

def data_grad(gradient, weight):
    chans, depth_n, height_n, width_n = gradient.shape
    padded = pad_space(gradient)
    summed = jnp.zeros((depth_n * height_n * width_n, weight.shape[4]), jnp.float32)
    for depth in range(3):
        for height in range(3):
            for across in range(3):
                window = padded[:, 2 - depth:2 - depth + depth_n, 2 - height:2 - height + height_n, 2 - across:2 - across + width_n].reshape(chans, -1)
                summed = summed + jnp.dot(window.T, weight[depth, height, across], preferred_element_type=jnp.float32)
    return summed

def reference(inputs, preact, cotangent, weight1, weight2):
    factor = 1.0 / jnp.sqrt(jnp.float32(NZ * Y * X))
    inputs_v = inputs.reshape(C, NZ, Y, X)
    preact_v = preact.reshape(C, NZ, Y, X)
    cot_v = cotangent.reshape(C, NZ, Y, X)
    hidden = jnp.maximum(preact_v, jnp.zeros((), preact.dtype))
    filter2_grad = filter_grad(hidden, cot_v) * factor
    unit_grad = data_grad(cot_v, weight2).T.reshape(C, NZ, Y, X)
    preact_grad = jnp.where(preact_v > 0, unit_grad, 0.0).astype(jnp.bfloat16)
    filter1_grad = filter_grad(inputs_v, preact_grad) * factor
    input_grad = data_grad(preact_grad, weight1).reshape(NZ, Y, X, C).astype(jnp.bfloat16)
    return (input_grad, filter1_grad, filter2_grad)
```

```python
import functools

import jax
import jax.numpy as jnp
from jax import lax
from jax.experimental import pallas as pl
from jax.experimental.pallas import tpu as pltpu
from jax.sharding import Mesh
from jax.sharding import PartitionSpec as P

AF = ("yh", "x", "core")
GZ = ("z", "yl")
SIZE = {"yh": 2, "x": 4, "core": 2, "z": 4, "yl": 2}
ROW = 32
CELLS = 1024
TAPS = 9
BLOCK = 32
WIDE = 128
DEPTH = 4
SRC = 4
DEEP = TAPS * BLOCK
K = SRC * DEEP
VMEM_BYTES = 48 * 1024 * 1024
NN = (((1,), (0,)), ((), ()))
NT = (((1,), (1,)), ((), ()))
F32 = jnp.float32
BF16 = jnp.bfloat16


def params():
    return pltpu.CompilerParams(vmem_limit_bytes=VMEM_BYTES)


def whole(count):
    return [pl.BlockSpec(memory_space=pltpu.VMEM)] * count


def from_ahead(value, axis, step):
    n = SIZE[axis]
    return lax.ppermute(value, axis, [(i, (i - step) % n) for i in range(n)])


def shape(dims, kind=BF16):
    return jax.ShapeDtypeStruct(dims, kind)


def regroup_kernel(w_ref, order_ref, own_ref, core_ref, far_ref):
    rows = w_ref[...]
    for block, target in enumerate(
        (own_ref, core_ref, far_ref.at[0], far_ref.at[1])
    ):
        picked = lax.dot_general(
            rows, order_ref[block * WIDE : (block + 1) * WIDE, :], NT, preferred_element_type=F32
        )
        target[...] = picked.astype(BF16)


def regroup(weight, order):
    rows = weight.reshape(27 * BLOCK, 512)
    one = shape((27 * BLOCK, WIDE))
    return pl.pallas_call(
        regroup_kernel,
        out_shape=(one, one, shape((2, 27 * BLOCK, WIDE))),
        in_specs=whole(2),
        out_specs=tuple(whole(3)),
        compiler_params=params(),
        cost_estimate=pl.CostEstimate(flops=2 * 864 * 512 * 512, bytes_accessed=2300000, transcendentals=0),
        name="regroup",
    )(rows, order)


def masks():
    lane = lax.broadcasted_iota(jnp.int32, (BLOCK, CELLS), 1)
    col = lane & (ROW - 1)
    one = lambda keep: jnp.where(keep, 1.0, 0.0).astype(BF16)
    return (
        one(col < ROW - 1),
        one(col > 0),
        one(lane < CELLS - ROW),
        one(lane >= ROW),
    )


def shift_plane(grads, plane, shifted, keep):
    left, right, top, bottom = keep
    for src in range(SRC):
        own_ref, rim_ref = grads[2 * src], grads[2 * src + 1]
        if plane == 0:
            mid = rim_ref[0]
        elif plane == DEPTH + 1:
            mid = rim_ref[1]
        else:
            mid = own_ref[plane - 1]
        across = (
            pltpu.roll(mid, CELLS - 1, 1) * left,
            mid,
            pltpu.roll(mid, 1, 1) * right,
        )
        for kx in range(3):
            rows = (
                pltpu.roll(across[kx], CELLS - ROW, 1) * top,
                across[kx],
                pltpu.roll(across[kx], ROW, 1) * bottom,
            )
            for ky in range(3):
                at = src * DEEP + (ky * 3 + kx) * BLOCK
                shifted[at : at + BLOCK, :] = rows[ky]


def taps_of(plane):
    return max(0, 2 - plane), min(3, DEPTH + 2 - plane)


def data_sums(grads, weights, turned, shifted, total):
    for kz in range(3):
        for src in range(SRC):
            block = weights[src][kz * DEEP : (kz + 1) * DEEP, :]
            shifted[0, src * DEEP : (src + 1) * DEEP, :WIDE] = block
        turned[kz * WIDE : (kz + 1) * WIDE, :] = shifted[0, :, :WIDE].T
    keep = masks()
    total[...] = jnp.zeros_like(total)
    for plane in range(DEPTH + 2):
        slot = shifted.at[plane % 2]
        shift_plane(grads, plane, slot, keep)
        low, high = taps_of(plane)
        first = plane - 2 + low
        for part in range(4):
            lanes = slice(part * 256, (part + 1) * 256)
            total[first * WIDE : (first + high - low) * WIDE, lanes] += lax.dot_general(
                turned[low * WIDE : high * WIDE, :], slot[:, lanes], NN, preferred_element_type=F32
            )


def data_by_channel_kernel(*refs):
    grads, weights, outs = refs[:8], refs[8:12], refs[12:16]
    turned, shifted, total = refs[16:]
    data_sums(grads, weights, turned, shifted, total)
    for dx in range(4):
        for plane in range(DEPTH):
            at = plane * WIDE + dx * BLOCK
            outs[dx][plane] = total[at : at + BLOCK, :].astype(BF16)


def data_by_row_kernel(place_ref, *refs):
    grads, weights, outs = refs[:8], refs[8:12], refs[12:16]
    turned, shifted, total = refs[16:]
    data_sums(grads, weights, turned, shifted, total)
    yh, x = place_ref[0], place_ref[1]
    for dx in range(4):
        for dyh in range(2):
            chunk = (yh + dyh) % 2 * 4 + (x + dx) % 4
            lanes = pl.ds(pl.multiple_of(chunk * WIDE, WIDE), WIDE)
            for plane in range(DEPTH):
                for block in range(4):
                    at = plane * WIDE + (dx + block) % 4 * BLOCK
                    outs[dx][dyh, plane, block * BLOCK : (block + 1) * BLOCK] = total[at : at + BLOCK, lanes].astype(BF16)


DATA_SCRATCH = [
    pltpu.VMEM((3 * WIDE, K), BF16),
    pltpu.VMEM((2, K, CELLS), BF16),
    pltpu.VMEM((DEPTH * WIDE, CELLS), F32),
]
DATA_COST = pl.CostEstimate(flops=2 * 27 * WIDE * WIDE * DEPTH * CELLS, bytes_accessed=3500000, transcendentals=0)


def data_by_channel(grads, weights):
    return pl.pallas_call(
        data_by_channel_kernel,
        out_shape=(shape((DEPTH, BLOCK, CELLS)),) * 4,
        in_specs=whole(12),
        out_specs=tuple(whole(4)),
        scratch_shapes=DATA_SCRATCH,
        compiler_params=params(),
        cost_estimate=DATA_COST,
        name="data_by_channel",
    )(*grads, *weights)


def data_by_row(place, grads, weights):
    return pl.pallas_call(
        data_by_row_kernel,
        out_shape=(shape((2, DEPTH, WIDE, WIDE)),) * 4,
        in_specs=[pl.BlockSpec(memory_space=pltpu.SMEM)] + whole(12),
        out_specs=tuple(whole(4)),
        scratch_shapes=DATA_SCRATCH,
        compiler_params=params(),
        cost_estimate=DATA_COST,
        name="data_by_row",
    )(place, *grads, *weights)


def filter_kernel(place_ref, *refs):
    grads, sources, outs = refs[:8], refs[8:12], refs[12:16]
    stacked, shifted, total = refs[16:]
    for dx in range(4):
        for plane in range(DEPTH):
            at = plane * WIDE + dx * BLOCK
            stacked[at : at + BLOCK, :] = sources[dx][plane]
    keep = masks()
    total[...] = jnp.zeros_like(total)
    for plane in range(DEPTH + 2):
        slot = shifted.at[plane % 2]
        shift_plane(grads, plane, slot, keep)
        low, high = taps_of(plane)
        first = plane - 2 + low
        for src in range(SRC):
            rows = slice(src * DEEP, (src + 1) * DEEP)
            part = lax.dot_general(
                slot[rows, :],
                stacked[first * WIDE : (first + high - low) * WIDE, :],
                NT,
                preferred_element_type=F32,
            )
            total[src * TAPS : (src + 1) * TAPS, :, :, low * WIDE : high * WIDE] += part.reshape(
                TAPS, 4, 8, (high - low) * WIDE
            )
    z = place_ref[2]
    for dz in range(4):
        rows = total[:, pl.ds((z + dz) % 4, 1), :, :]
        outs[dz][...] = rows.reshape(SRC * TAPS * 8, 3 * WIDE).astype(BF16)


def filter_sums(place, grads, sources):
    return pl.pallas_call(
        filter_kernel,
        out_shape=(shape((SRC * TAPS * 8, 3 * WIDE)),) * 4,
        in_specs=[pl.BlockSpec(memory_space=pltpu.SMEM)] + whole(12),
        out_specs=tuple(whole(4)),
        scratch_shapes=[
            pltpu.VMEM((DEPTH * WIDE, CELLS), BF16),
            pltpu.VMEM((2, K, CELLS), BF16),
            pltpu.VMEM((SRC * TAPS, 4, 8, 3 * WIDE), F32),
        ],
        compiler_params=params(),
        cost_estimate=DATA_COST,
        name="filter_sums",
    )(place, *grads, *sources)


def gather_outputs(own):
    core = from_ahead(own, "core", 1)
    far = from_ahead(own, "yh", 1)
    return own, core, far, from_ahead(far, "core", 1)


def gather_inputs(own):
    return (own,) + tuple(from_ahead(own, "x", d) for d in (1, 2, 3))


def sum_ahead(blocks, axis):
    total = blocks[0].astype(F32)
    for d in range(1, 4):
        total = total + from_ahead(blocks[d], axis, -d).astype(F32)
    return total


def gather_weight(weight, order):
    own, core, far = regroup(weight, order)
    far = from_ahead(far, "yh", 1)
    return own, from_ahead(core, "core", 1), far[0], from_ahead(far[1], "core", 1)


def gather_grads(own):
    low = lax.ppermute(own[DEPTH - 1 :], GZ, [(i, i + 1) for i in range(7)])
    high = lax.ppermute(own[:1], GZ, [(i + 1, i) for i in range(7)])
    rim = jnp.concatenate([low, high], axis=0)
    grads = []
    for a, b in zip(gather_outputs(own), gather_outputs(rim)):
        grads += [a, b]
    return grads


def finish_filter(parts, order, yl, factor):
    part = sum_ahead(parts, "z").astype(BF16)
    part = part.reshape(2, 2, TAPS, 2, 4, 3 * WIDE)
    mine = lax.dynamic_index_in_dim(part, yl, 3, keepdims=False)
    other = lax.dynamic_index_in_dim(part, 1 - yl, 3, keepdims=False)
    part = (mine.astype(F32) + from_ahead(other, "yl", 1).astype(F32)).astype(BF16)
    near = part[0]
    far = from_ahead(part[1], "yh", 1)
    give = jnp.stack([near[1], far[1]])
    got = from_ahead(give, "core", 1)
    full = jnp.stack([near[0], got[0], far[0], got[1]])
    full = full.reshape(SRC, TAPS * 4, 3, WIDE).transpose(2, 1, 0, 3).reshape(3 * TAPS * 4, SRC * WIDE)
    out = jnp.dot(full, order, preferred_element_type=F32)
    return out.reshape(3, 3, 3, 4, SRC * WIDE) * factor


def place_kernel(core_ref, a, b, c, d, order_ref, out_ref, rows):
    start = pl.multiple_of(core_ref[0] * 64, 64)
    for plane in range(DEPTH):
        total = None
        for src, ref in enumerate((a, b, c, d)):
            part = lax.dot_general(
                ref[plane].T,
                order_ref[src * WIDE : (src + 1) * WIDE, :],
                NN,
                preferred_element_type=F32,
            )
            total = part if total is None else total + part
        rows[...] = total
        out_ref[plane] = rows[pl.ds(start, 64), :].astype(BF16)


def finish_image(parts, order, core):
    part = sum_ahead(parts, "x").astype(BF16)
    near = part[0]
    far = from_ahead(part[1], "yh", 1)
    near_got = from_ahead(near, "core", 1)
    far_got = from_ahead(far, "core", 1)
    out = pl.pallas_call(
        place_kernel,
        out_shape=shape((DEPTH, 64, 512)),
        in_specs=[pl.BlockSpec(memory_space=pltpu.SMEM)] + whole(5),
        out_specs=whole(1)[0],
        scratch_shapes=[pltpu.VMEM((WIDE, 512), F32)],
        compiler_params=params(),
        name="place",
    )(core.reshape(1), near, near_got, far, far_got, order)
    return out.reshape(DEPTH, 2, ROW, 512)


def order_matrix(yh, x, core):
    row = lax.broadcasted_iota(jnp.int32, (512, 512), 0)
    dyh, dcore, dx, r = row // 256, row // 128 % 2, row // 32 % 4, row % 32
    channel = ((yh + dyh) % 2) * 256 + ((x + dx) % 4) * 64 + ((core + dcore) % 2) * 32 + r
    lane = lax.broadcasted_iota(jnp.int32, (512, 512), 1)
    return jnp.where(channel == lane, 1.0, 0.0).astype(BF16)


def body(inputs, preact, cotangent, weight1, weight2):
    yh, x, core = (lax.axis_index(a) for a in AF)
    z, yl = (lax.axis_index(a) for a in GZ)
    place = jnp.stack([yh, x, z]).astype(jnp.int32)
    factor = 1.0 / jnp.sqrt(F32(32 * CELLS))
    order = order_matrix(yh, x, core)

    cot = cotangent.transpose(1, 0, 2)
    weights2 = gather_weight(weight2, order)
    grads2 = gather_grads(cot)
    pre = preact.transpose(1, 0, 2)
    hidden = gather_inputs(jnp.maximum(pre, jnp.zeros((), BF16)))
    sources = gather_inputs(inputs.transpose(1, 0, 2))
    weights1 = gather_weight(weight1, order)

    unit = sum_ahead(data_by_channel(grads2, weights2), "x")
    filter2_parts = filter_sums(place, grads2, hidden)
    preact_grad = jnp.where(pre > 0, unit, 0.0).astype(BF16)
    grads1 = gather_grads(preact_grad)
    image_parts = data_by_row(place, grads1, weights1)
    filter1_parts = filter_sums(place, grads1, sources)
    input_grad = finish_image(image_parts, order, core)
    return (
        input_grad,
        finish_filter(filter1_parts, order, yl, factor),
        finish_filter(filter2_parts, order, yl, factor),
    )


def solution(mesh):
    fine = Mesh(mesh.devices.reshape(2, 4, 2, 4, 2), AF + GZ)
    placed = (
        P(AF, GZ, None),
        P(AF, GZ, None),
        P(AF, GZ, None),
        P(None, None, None, AF, None),
        P(None, None, None, AF, None),
    )
    return jax.shard_map(
        body,
        mesh=fine,
        in_specs=placed,
        out_specs=(
            P(GZ, AF, None, None),
            P(None, None, None, AF + GZ, None),
            P(None, None, None, AF + GZ, None),
        ),
        check_vma=False,
    )
```

```python
import functools

import jax
import jax.numpy as jnp
from jax import lax
from jax.experimental import pallas as pl
from jax.experimental.pallas import tpu as pltpu
from jax.sharding import Mesh
from jax.sharding import PartitionSpec as P

AF = ("yh", "x", "core")
GZ = ("z", "yl")
SIZE = {"yh": 2, "x": 4, "core": 2, "z": 4, "yl": 2}
ROW = 32
CELLS = 1024
TAPS = 9
BLOCK = 32
WIDE = 128
DEPTH = 4
SRC = 4
DEEP = TAPS * BLOCK
K = SRC * DEEP
VMEM_BYTES = 48 * 1024 * 1024
NN = (((1,), (0,)), ((), ()))
NT = (((1,), (1,)), ((), ()))
F32 = jnp.float32
BF16 = jnp.bfloat16


def params():
    return pltpu.CompilerParams(vmem_limit_bytes=VMEM_BYTES)


def whole(count):
    return [pl.BlockSpec(memory_space=pltpu.VMEM)] * count


def from_ahead(value, axis, step):
    n = SIZE[axis]
    return lax.ppermute(value, axis, [(i, (i - step) % n) for i in range(n)])


def shape(dims, kind=BF16):
    return jax.ShapeDtypeStruct(dims, kind)


def picks(place_ref, dyh, dcore, relative):
    yh, x, core = place_ref[0], place_ref[1], place_ref[2]
    row = lax.broadcasted_iota(jnp.int32, (WIDE, 512), 0)
    lane = lax.broadcasted_iota(jnp.int32, (WIDE, 512), 1)
    column = row // BLOCK
    if relative:
        column = (column + x) % 4
    channel = (yh + dyh) % 2 * 256 + (core + dcore) % 2 * BLOCK + column * 64 + row % BLOCK
    return jnp.where(channel == lane, 1.0, 0.0).astype(BF16)


def regroup_kernel(place_ref, w_ref, own_ref, core_ref, far_ref):
    rows = w_ref[...]
    for block, target in enumerate((own_ref, core_ref, far_ref.at[0], far_ref.at[1])):
        order = picks(place_ref, block // 2, block % 2, True)
        picked = lax.dot_general(rows, order, NT, preferred_element_type=F32)
        target[...] = picked.astype(BF16)


def regroup(place, weight):
    rows = weight.reshape(27 * BLOCK, 512)
    one = shape((27 * BLOCK, WIDE))
    return pl.pallas_call(
        regroup_kernel,
        out_shape=(one, one, shape((2, 27 * BLOCK, WIDE))),
        in_specs=[pl.BlockSpec(memory_space=pltpu.SMEM)] + whole(1),
        out_specs=tuple(whole(3)),
        compiler_params=params(),
        cost_estimate=pl.CostEstimate(flops=2 * 864 * 512 * 512, bytes_accessed=1800000, transcendentals=0),
        name="regroup",
    )(place, rows)


def masks():
    lane = lax.broadcasted_iota(jnp.int32, (BLOCK, CELLS), 1)
    col = lane & (ROW - 1)
    one = lambda keep: jnp.where(keep, 1.0, 0.0).astype(BF16)
    return (
        one(col < ROW - 1),
        one(col > 0),
        one(lane < CELLS - ROW),
        one(lane >= ROW),
    )


def shift_plane(grads, plane, shifted, keep):
    left, right, top, bottom = keep
    for src in range(SRC):
        own_ref, rim_ref = grads[2 * src], grads[2 * src + 1]
        if plane == 0:
            mid = rim_ref[0]
        elif plane == DEPTH + 1:
            mid = rim_ref[1]
        else:
            mid = own_ref[plane - 1]
        across = (
            pltpu.roll(mid, CELLS - 1, 1) * left,
            mid,
            pltpu.roll(mid, 1, 1) * right,
        )
        for kx in range(3):
            rows = (
                pltpu.roll(across[kx], CELLS - ROW, 1) * top,
                across[kx],
                pltpu.roll(across[kx], ROW, 1) * bottom,
            )
            for ky in range(3):
                at = src * DEEP + (ky * 3 + kx) * BLOCK
                shifted[at : at + BLOCK, :] = rows[ky]


def taps_of(plane):
    return max(0, 2 - plane), min(3, DEPTH + 2 - plane)


def data_sums(grads, weights, turned, shifted, total):
    for kz in range(3):
        for src in range(SRC):
            block = weights[src][kz * DEEP : (kz + 1) * DEEP, :]
            shifted[0, src * DEEP : (src + 1) * DEEP, :WIDE] = block
        turned[kz * WIDE : (kz + 1) * WIDE, :] = shifted[0, :, :WIDE].T
    keep = masks()
    for plane in range(DEPTH + 2):
        slot = shifted.at[plane % 2]
        shift_plane(grads, plane, slot, keep)
        low, high = taps_of(plane)
        for part in range(4):
            lanes = slice(part * 256, (part + 1) * 256)
            part = lax.dot_general(
                turned[low * WIDE : high * WIDE, :], slot[:, lanes], NN, preferred_element_type=F32
            )
            for kz in range(low, high):
                at = (plane - 2 + kz) * WIDE
                piece = part[(kz - low) * WIDE : (kz - low + 1) * WIDE]
                if kz < 2:
                    piece = piece + total[at : at + WIDE, lanes]
                total[at : at + WIDE, lanes] = piece


def data_by_channel_kernel(*refs):
    grads, weights, outs = refs[:8], refs[8:12], refs[12:16]
    total = refs[-1]
    data_sums(grads, weights, *refs[16:])
    for dx in range(4):

        @pl.loop(0, DEPTH)
        def _(plane):
            at = pl.multiple_of(plane * WIDE + dx * BLOCK, BLOCK)
            outs[dx][plane] = total[pl.ds(at, BLOCK), :].astype(BF16)


def data_by_row_kernel(place_ref, *refs):
    grads, weights, outs = refs[:8], refs[8:12], refs[12:16]
    total = refs[-1]
    data_sums(grads, weights, *refs[16:])
    yh, x = place_ref[0], place_ref[1]
    for dx in range(4):

        @pl.loop(0, 2 * DEPTH)
        def _(step):
            dyh, plane = step // DEPTH, step % DEPTH
            chunk = (yh + dyh) % 2 * 4 + (x + dx) % 4
            lanes = pl.ds(pl.multiple_of(chunk * WIDE, WIDE), WIDE)
            for block in range(4):
                at = pl.multiple_of(plane * WIDE + (dx + block) % 4 * BLOCK, BLOCK)
                outs[dx][dyh, plane, block * BLOCK : (block + 1) * BLOCK] = total[pl.ds(at, BLOCK), lanes].astype(BF16)


DATA_SCRATCH = [
    pltpu.VMEM((3 * WIDE, K), BF16),
    pltpu.VMEM((2, K, CELLS), BF16),
    pltpu.VMEM((DEPTH * WIDE, CELLS), F32),
]
DATA_COST = pl.CostEstimate(flops=2 * 27 * WIDE * WIDE * DEPTH * CELLS, bytes_accessed=3500000, transcendentals=0)


def data_by_channel(grads, weights):
    return pl.pallas_call(
        data_by_channel_kernel,
        out_shape=(shape((DEPTH, BLOCK, CELLS)),) * 4,
        in_specs=whole(12),
        out_specs=tuple(whole(4)),
        scratch_shapes=DATA_SCRATCH,
        compiler_params=params(),
        cost_estimate=DATA_COST,
        name="data_by_channel",
    )(*grads, *weights)


def data_by_row(place, grads, weights):
    return pl.pallas_call(
        data_by_row_kernel,
        out_shape=(shape((2, DEPTH, WIDE, WIDE)),) * 4,
        in_specs=[pl.BlockSpec(memory_space=pltpu.SMEM)] + whole(12),
        out_specs=tuple(whole(4)),
        scratch_shapes=DATA_SCRATCH,
        compiler_params=params(),
        cost_estimate=DATA_COST,
        name="data_by_row",
    )(place, *grads, *weights)


def filter_kernel(place_ref, *refs):
    grads, sources, out_ref = refs[:8], refs[8:9], refs[9]
    stacked, shifted, total = refs[10:]
    for x in range(4):
        for plane in range(DEPTH):
            at = plane * WIDE + x * BLOCK
            stacked[at : at + BLOCK, :] = sources[0][x, plane]

    keep = masks()
    for plane in range(DEPTH + 2):
        slot = shifted.at[plane % 2]
        shift_plane(grads, plane, slot, keep)
        low, high = taps_of(plane)
        first = plane - 2 + low
        for src in range(SRC):
            part = lax.dot_general(
                slot[src * DEEP : (src + 1) * DEEP, :],
                stacked[first * WIDE : (first + high - low) * WIDE, :],
                NT,
                preferred_element_type=F32,
            )
            for kz in range(low, high):
                piece = part[:, (kz - low) * WIDE : (kz - low + 1) * WIDE]
                lanes = slice(kz * WIDE, (kz + 1) * WIDE)
                if plane != 2 - kz:
                    piece = piece + total[src, :, lanes]
                total[src, :, lanes] = piece

    upper = lax.broadcasted_iota(jnp.int32, (18, 8, 3 * WIDE), 1) < 4

    for z in range(4):
        rows = total[...].reshape(18, 2, 4, 8, 3 * WIDE)
        one, two = rows[:, 0, z], rows[:, 1, z]
        low = jnp.where(upper, one, pltpu.roll(two, 4, 1))
        high = jnp.where(upper, pltpu.roll(one, 4, 1), two)
        out_ref[2 * z] = low.reshape(18 * 8, 3 * WIDE).astype(BF16)
        out_ref[2 * z + 1] = high.reshape(18 * 8, 3 * WIDE).astype(BF16)


def filter_sums(place, grads, sources):
    return pl.pallas_call(
        filter_kernel,
        out_shape=shape((8, SRC * TAPS * 4, 3 * WIDE)),
        in_specs=[pl.BlockSpec(memory_space=pltpu.SMEM)] + whole(9),
        out_specs=whole(1)[0],
        scratch_shapes=[
            pltpu.VMEM((DEPTH * WIDE, CELLS), BF16),
            pltpu.VMEM((2, K, CELLS), BF16),
            pltpu.VMEM((SRC, DEEP, 3 * WIDE), F32),
        ],
        compiler_params=params(),
        cost_estimate=DATA_COST,
        name="filter_sums",
    )(place, *grads, sources)


def gather_outputs(own):
    core = from_ahead(own, "core", 1)
    far = from_ahead(own, "yh", 1)
    return own, core, far, from_ahead(far, "core", 1)


def sum_ahead(blocks, axis):
    total = blocks[0].astype(F32)
    for d in range(1, 4):
        total = total + from_ahead(blocks[d], axis, -d).astype(F32)
    return total


def gather_weight(place, weight):
    own, core, far = regroup(place, weight)
    far = from_ahead(far, "yh", 1)
    return own, from_ahead(core, "core", 1), far[0], from_ahead(far[1], "core", 1)


def gather_grads(own):
    low = lax.ppermute(own[DEPTH - 1 :], GZ, [(i, i + 1) for i in range(7)])
    high = lax.ppermute(own[:1], GZ, [(i + 1, i) for i in range(7)])
    rim = jnp.concatenate([low, high], axis=0)
    grads = []
    for a, b in zip(gather_outputs(own), gather_outputs(rim)):
        grads += [a, b]
    return grads


def place_filters_kernel(place_ref, factor_ref, a, b, c, d, out_ref):
    for src, ref in enumerate((a, b, c, d)):
        order = picks(place_ref, src // 2, src % 2, False)
        for kz in range(3):
            part = lax.dot_general(
                ref[:, kz * WIDE : (kz + 1) * WIDE], order, NN, preferred_element_type=F32
            )
            if src:
                part = part + out_ref[kz]
            if src == 3:
                part = part * factor_ref[0]
            out_ref[kz] = part


def finish_filters(place, sums, factor):
    count = len(sums)
    rows = jnp.stack([one.reshape(2, 2, TAPS * 4, 3 * WIDE) for one in sums], axis=2)
    far = from_ahead(rows[1], "yh", 1)
    got = from_ahead(jnp.stack([rows[0, 1], far[1]]), "core", 1)
    blocks = [rows[0, 0], got[0], far[0], got[1]]
    out = pl.pallas_call(
        place_filters_kernel,
        out_shape=shape((3, count * TAPS * 4, 512), F32),
        in_specs=[pl.BlockSpec(memory_space=pltpu.SMEM)] * 2 + whole(4),
        out_specs=whole(1)[0],
        compiler_params=params(),
        name="place_filters",
    )(place, factor.reshape(1), *[one.reshape(count * TAPS * 4, 3 * WIDE) for one in blocks])
    out = out.reshape(3, count, 3, 3, 4, 512)
    return [out[:, i] for i in range(count)]


def place_kernel(place_ref, a, b, c, d, out_ref, rows):
    start = pl.multiple_of(place_ref[2] * 64, 64)
    orders = [picks(place_ref, src // 2, src % 2, True) for src in range(SRC)]
    for plane in range(DEPTH):
        total = None
        for order, ref in zip(orders, (a, b, c, d)):
            part = lax.dot_general(ref[plane].T, order, NN, preferred_element_type=F32)
            total = part if total is None else total + part
        rows[...] = total
        out_ref[plane] = rows[pl.ds(start, 64), :].astype(BF16)


def finish_image(parts, place):
    part = sum_ahead(parts, "x").astype(BF16)
    near = part[0]
    far = from_ahead(part[1], "yh", 1)
    near_got = from_ahead(near, "core", 1)
    far_got = from_ahead(far, "core", 1)
    out = pl.pallas_call(
        place_kernel,
        out_shape=shape((DEPTH, 64, 512)),
        in_specs=[pl.BlockSpec(memory_space=pltpu.SMEM)] + whole(4),
        out_specs=whole(1)[0],
        scratch_shapes=[pltpu.VMEM((WIDE, 512), F32)],
        compiler_params=params(),
        name="place",
    )(place, near, near_got, far, far_got)
    return out.reshape(DEPTH, 2, ROW, 512)


def after(place, done):
    return lax.optimization_barrier((place, done))[0]


def body(inputs, preact, cotangent, weight1, weight2):
    place = jnp.stack([lax.axis_index(a) for a in AF]).astype(jnp.int32)
    factor = 1.0 / jnp.sqrt(F32(32 * CELLS))

    cot = cotangent.transpose(1, 0, 2)
    weights2 = gather_weight(place, weight2)
    grads2 = gather_grads(cot)
    pre = preact.transpose(1, 0, 2)
    hidden = lax.all_gather(jnp.maximum(pre, jnp.zeros((), BF16)), "x", axis=0)
    sources = lax.all_gather(inputs.transpose(1, 0, 2), "x", axis=0)

    unit_parts = data_by_channel(grads2, weights2)
    later = after(place, unit_parts[0])
    weights1 = gather_weight(later, weight1)
    filter2_parts = filter_sums(later, grads2, hidden)
    filter2_sum = lax.psum_scatter(filter2_parts, GZ, scatter_dimension=0)
    unit = sum_ahead(unit_parts, "x")
    preact_grad = jnp.where(pre > 0, unit, 0.0).astype(BF16)
    grads1 = gather_grads(preact_grad)
    filter1_parts = filter_sums(place, grads1, sources)
    filter1_sum = lax.psum_scatter(filter1_parts, GZ, scatter_dimension=0)
    image_parts = data_by_row(after(place, filter1_parts), grads1, weights1)
    input_grad = finish_image(image_parts, place)
    filter1_grad, filter2_grad = finish_filters(place, [filter1_sum, filter2_sum], factor)
    return input_grad, filter1_grad, filter2_grad


def solution(mesh):
    fine = Mesh(mesh.devices.reshape(2, 4, 2, 4, 2), AF + GZ)
    placed = (
        P(AF, GZ, None),
        P(AF, GZ, None),
        P(AF, GZ, None),
        P(None, None, None, AF, None),
        P(None, None, None, AF, None),
    )
    return jax.shard_map(
        body,
        mesh=fine,
        in_specs=placed,
        out_specs=(
            P(GZ, AF, None, None),
            P(None, None, None, AF + GZ, None),
            P(None, None, None, AF + GZ, None),
        ),
        check_vma=False,
    )
```

```python
import functools

import jax
import jax.numpy as jnp
from jax import lax
from jax.experimental import pallas as pl
from jax.experimental.pallas import tpu as pltpu
from jax.sharding import Mesh
from jax.sharding import PartitionSpec as P

AF = ("yh", "x", "core")
GZ = ("z", "yl")
SIZE = {"yh": 2, "x": 4, "core": 2, "z": 4, "yl": 2}
ROW = 32
CELLS = 1024
TAPS = 9
BLOCK = 32
WIDE = 128
DEPTH = 4
SRC = 4
DEEP = TAPS * BLOCK
K = SRC * DEEP
VMEM_BYTES = 20 * 1024 * 1024
NN = (((1,), (0,)), ((), ()))
NT = (((1,), (1,)), ((), ()))
COST = pl.CostEstimate(flops=1000, bytes_accessed=1000, transcendentals=0)
F32 = jnp.float32
BF16 = jnp.bfloat16


def params():
    return pltpu.CompilerParams(vmem_limit_bytes=VMEM_BYTES)


def whole(count):
    return [pl.BlockSpec(memory_space=pltpu.VMEM)] * count


def from_ahead(value, axis, step):
    n = SIZE[axis]
    return lax.ppermute(value, axis, [(i, (i - step) % n) for i in range(n)])


def shape(dims, kind=BF16):
    return jax.ShapeDtypeStruct(dims, kind)


def picks(place_ref, dyh, dcore):
    yh, x, core = place_ref[0], place_ref[1], place_ref[2]
    row = lax.broadcasted_iota(jnp.int32, (WIDE, 512), 0)
    lane = lax.broadcasted_iota(jnp.int32, (WIDE, 512), 1)
    column = (row // BLOCK + x) % 4
    channel = (yh + dyh) % 2 * 256 + (core + dcore) % 2 * BLOCK + column * 64 + row % BLOCK
    return jnp.where(channel == lane, 1.0, 0.0).astype(BF16)


def orders_kernel(place_ref, out_ref):
    for src in range(SRC):
        out_ref[src * WIDE : (src + 1) * WIDE, :] = picks(place_ref, src // 2, src % 2)


def make_orders(place):
    return pl.pallas_call(
        orders_kernel,
        out_shape=shape((512, 512)),
        in_specs=[pl.BlockSpec(memory_space=pltpu.SMEM)],
        out_specs=whole(1)[0],
        compiler_params=params(),
        cost_estimate=COST,
        name="orders",
    )(place)


def regroup_kernel(w_ref, order_ref, own_ref, core_ref, far_ref):
    rows = w_ref[...]
    for block, target in enumerate((own_ref, core_ref, far_ref.at[0], far_ref.at[1])):
        order = order_ref[block * WIDE : (block + 1) * WIDE, :]
        picked = lax.dot_general(rows, order, NT, preferred_element_type=F32)
        target[...] = picked.astype(BF16)


def regroup(weight, order):
    rows = weight.reshape(27 * BLOCK, 512)
    one = shape((27 * BLOCK, WIDE))
    return pl.pallas_call(
        regroup_kernel,
        out_shape=(one, one, shape((2, 27 * BLOCK, WIDE))),
        in_specs=whole(2),
        out_specs=tuple(whole(3)),
        compiler_params=params(),
        cost_estimate=COST,
        name="regroup",
    )(rows, order)


def masks():
    lane = lax.broadcasted_iota(jnp.int32, (BLOCK, CELLS), 1)
    col = lane & (ROW - 1)
    one = lambda keep: jnp.where(keep, 1.0, 0.0).astype(BF16)
    return (
        one(col < ROW - 1),
        one(col > 0),
        one(lane < CELLS - ROW),
        one(lane >= ROW),
    )


def shift_plane(refs, shifted, keep):
    left, right, top, bottom = keep
    for src, ref in enumerate(refs):
        mid = ref[...]
        across = (
            pltpu.roll(mid, CELLS - 1, 1) * left,
            mid,
            pltpu.roll(mid, 1, 1) * right,
        )
        for kx in range(3):
            rows = (
                pltpu.roll(across[kx], CELLS - ROW, 1) * top,
                across[kx],
                pltpu.roll(across[kx], ROW, 1) * bottom,
            )
            for ky in range(3):
                at = src * DEEP + (ky * 3 + kx) * BLOCK
                shifted[at : at + BLOCK, :] = rows[ky]


def four(own, far, got):
    return own, got.at[0], far, got.at[1]


def plane_refs(grads, plane):
    at = {0: DEPTH, DEPTH + 1: DEPTH + 1}.get(plane, plane - 1)
    return [ref.at[at] for ref in four(*grads)]


def taps_of(plane):
    return max(0, 2 - plane), min(3, DEPTH + 2 - plane)


def data_sums(grads, weights, turned, shifted, total):
    own, far, got = weights
    for kz in range(3):
        rows = slice(kz * DEEP, (kz + 1) * DEEP)
        for src, block in enumerate((own[rows], got[0, rows], far[0, rows], got[1, rows])):
            shifted[0, src * DEEP : (src + 1) * DEEP, :WIDE] = block
        turned[kz * WIDE : (kz + 1) * WIDE, :] = shifted[0, :, :WIDE].T
    keep = masks()
    for plane in range(DEPTH + 2):
        slot = shifted.at[plane % 2]
        shift_plane(plane_refs(grads, plane), slot, keep)
        low, high = taps_of(plane)
        for part in range(4):
            lanes = slice(part * 256, (part + 1) * 256)
            part = lax.dot_general(
                turned[low * WIDE : high * WIDE, :], slot[:, lanes], NN, preferred_element_type=F32
            )
            for kz in range(low, high):
                at = (plane - 2 + kz) * WIDE
                piece = part[(kz - low) * WIDE : (kz - low + 1) * WIDE]
                if kz < 2:
                    piece = piece + total[at : at + WIDE, lanes]
                total[at : at + WIDE, lanes] = piece


def data_by_channel_kernel(*refs):
    grads, weights, outs = refs[:3], refs[3:6], refs[6:10]
    total = refs[-1]
    data_sums(grads, weights, *refs[10:])
    for dx in range(4):

        @pl.loop(0, DEPTH)
        def _(plane):
            at = pl.multiple_of(plane * WIDE + dx * BLOCK, BLOCK)
            outs[dx][plane] = total[pl.ds(at, BLOCK), :].astype(BF16)


def data_by_row_kernel(place_ref, *refs):
    grads, weights, outs = refs[:3], refs[3:6], refs[6:10]
    total = refs[-1]
    data_sums(grads, weights, *refs[10:])
    yh, x = place_ref[0], place_ref[1]
    for dx in range(4):

        @pl.loop(0, 2 * DEPTH)
        def _(step):
            dyh, plane = step // DEPTH, step % DEPTH
            chunk = (yh + dyh) % 2 * 4 + (x + dx) % 4
            lanes = pl.ds(pl.multiple_of(chunk * WIDE, WIDE), WIDE)
            for block in range(4):
                at = pl.multiple_of(plane * WIDE + (dx + block) % 4 * BLOCK, BLOCK)
                outs[dx][dyh, plane, block * BLOCK : (block + 1) * BLOCK] = total[pl.ds(at, BLOCK), lanes].astype(BF16)


DATA_SCRATCH = [
    pltpu.VMEM((3 * WIDE, K), BF16),
    pltpu.VMEM((2, K, CELLS), BF16),
    pltpu.VMEM((DEPTH * WIDE, CELLS), F32),
]


def data_by_channel(grads, weights):
    return pl.pallas_call(
        data_by_channel_kernel,
        out_shape=(shape((DEPTH, BLOCK, CELLS)),) * 4,
        in_specs=whole(6),
        out_specs=tuple(whole(4)),
        scratch_shapes=DATA_SCRATCH,
        compiler_params=params(),
        cost_estimate=COST,
        name="data_by_channel",
    )(*grads, *weights)


def data_by_row(place, grads, weights):
    return pl.pallas_call(
        data_by_row_kernel,
        out_shape=(shape((2, DEPTH, WIDE, WIDE)),) * 4,
        in_specs=[pl.BlockSpec(memory_space=pltpu.SMEM)] + whole(6),
        out_specs=tuple(whole(4)),
        scratch_shapes=DATA_SCRATCH,
        compiler_params=params(),
        cost_estimate=COST,
        name="data_by_row",
    )(place, *grads, *weights)


def add_products(total, slot, sources, low, high, fresh):
    for src in range(SRC):
        part = lax.dot_general(
            slot[src * DEEP : (src + 1) * DEEP, :], sources, NT, preferred_element_type=F32
        )
        for kz in range(low, high):
            piece = part[:, (kz - low) * WIDE : (kz - low + 1) * WIDE]
            lanes = slice(kz * WIDE, (kz + 1) * WIDE)
            piece = piece.reshape(TAPS, 4, 8, WIDE)
            rows = slice(src * TAPS, (src + 1) * TAPS)
            if not fresh(kz):
                piece = piece + total[rows, :, :, lanes]
            total[rows, :, :, lanes] = piece


def filter_total(grads, sources, first_plane, stacked, shifted, total):
    for dx in range(4):
        for plane in range(DEPTH):
            at = plane * WIDE + dx * BLOCK
            stacked[at : at + BLOCK, :] = sources[dx][first_plane + plane]
    keep = masks()
    for plane in range(DEPTH + 2):
        slot = shifted.at[plane % 2]
        shift_plane(plane_refs(grads, plane), slot, keep)
        low, high = taps_of(plane)
        first = plane - 2 + low
        rows = stacked[first * WIDE : (first + high - low) * WIDE, :]
        add_products(total, slot, rows, low, high, lambda kz: plane == 2 - kz)


def second_filter_kernel(place_ref, *refs):
    filter_total(refs[:3], refs[3:7], 0, *refs[8:])
    for z in range(4):
        low, high = rows_of(refs[-1], z)
        refs[7][z, 0], refs[7][z, 1] = low, high


def first_filter_kernel(place_ref, *refs):
    filter_total(refs[:3], refs[3:7], DEPTH, *refs[11:])
    for dz in range(4):
        low, high = rows_of(refs[-1], (place_ref[3] + dz) % 4)
        refs[7 + dz][0], refs[7 + dz][1] = low, high


def rows_of(total, z):
    upper = lax.broadcasted_iota(jnp.int32, (18, 8, 3 * WIDE), 1) < 4
    rows = total[:, pl.ds(z, 1), :, :].reshape(18, 2, 8, 3 * WIDE)
    one, two = rows[:, 0], rows[:, 1]
    low = jnp.where(upper, one, pltpu.roll(two, 4, 1))
    high = jnp.where(upper, pltpu.roll(one, 4, 1), two)
    return [half.reshape(18 * 8, 3 * WIDE).astype(BF16) for half in (low, high)]


def filter_sums(kernel, out_shape, *args):
    return pl.pallas_call(
        kernel,
        out_shape=out_shape,
        in_specs=[pl.BlockSpec(memory_space=pltpu.SMEM)] + whole(len(args) - 1),
        out_specs=jax.tree.map(lambda _: whole(1)[0], out_shape),
        scratch_shapes=[
            pltpu.VMEM((DEPTH * WIDE, CELLS), BF16),
            pltpu.VMEM((2, K, CELLS), BF16),
            pltpu.VMEM((SRC * TAPS, 4, 8, 3 * WIDE), F32),
        ],
        compiler_params=params(),
        cost_estimate=COST,
        name="filter_sums",
    )(*args)


def both_cores(near, far):
    return from_ahead(jnp.stack([near, far]), "core", 1)


def moved_ahead(blocks, axis):
    return [blocks[0]] + [from_ahead(blocks[d], axis, -d) for d in range(1, 4)]


def total_of(blocks):
    return sum(block.astype(F32) for block in blocks)


def halo(last, first):
    low = lax.ppermute(last, GZ, [(i, i + 1) for i in range(7)])
    high = lax.ppermute(first, GZ, [(i + 1, i) for i in range(7)])
    return low, high


def sum_yl(part):
    yl = lax.axis_index("yl")
    mine = lax.dynamic_index_in_dim(part, yl, 0, keepdims=False)
    other = lax.dynamic_index_in_dim(part, 1 - yl, 0, keepdims=False)
    return total_of([mine, from_ahead(other, "yl", 1)]).astype(BF16)


def place_filters_kernel(factor_ref, order_ref, own_ref, far_ref, got_ref, first_ref, second_ref):
    orders = [order_ref[src * WIDE : (src + 1) * WIDE, :] for src in range(SRC)]
    for index, out_ref in enumerate((first_ref, second_ref)):
        for kz in range(3):
            lanes = slice(kz * WIDE, (kz + 1) * WIDE)
            total = None
            for order, rows in zip(
                orders,
                (own_ref[index, :, lanes], got_ref[0, index, :, lanes], far_ref[index, :, lanes], got_ref[1, index, :, lanes]),
            ):
                part = lax.dot_general(rows, order, NN, preferred_element_type=F32)
                total = part if total is None else total + part
            total = total * factor_ref[0]
            for tap in range(TAPS):
                out_ref[kz * TAPS + tap] = total[tap * 4 : (tap + 1) * 4]


def finish_filters(order, sums, factor):
    rows = sums.reshape(2, 2, 2, TAPS * 4, 3 * WIDE).transpose(1, 2, 0, 3, 4)
    far = from_ahead(rows[1], "yh", 1)
    got = both_cores(rows[0, 1], far[1])
    outs = pl.pallas_call(
        place_filters_kernel,
        out_shape=(shape((27, 4, 512), F32),) * 2,
        in_specs=[pl.BlockSpec(memory_space=pltpu.SMEM)] + whole(4),
        out_specs=tuple(whole(2)),
        compiler_params=params(),
        cost_estimate=COST,
        name="place_filters",
    )(factor.reshape(1), order, rows[0, 0], far[0], got)
    return [out.reshape(3, 3, 3, 4, 512) for out in outs]


def place_kernel(place_ref, order_ref, own_ref, far_ref, got_ref, out_ref):
    upper = place_ref[2] == 1
    for pair in range(DEPTH // 2):
        halves = []
        for plane in (2 * pair, 2 * pair + 1):
            rows = jnp.concatenate([ref[plane] for ref in four(own_ref, far_ref, got_ref)], axis=0)
            halves.append(jnp.where(upper, rows[:, 64:], rows[:, :64]))
        cells = jnp.concatenate(halves, axis=1).T
        part = lax.dot_general(cells, order_ref[...], NN, preferred_element_type=F32).astype(BF16)
        out_ref[2 * pair], out_ref[2 * pair + 1] = part[:64], part[64:]


def finish_image(part, place, order):
    near = part[0]
    far = from_ahead(part[1], "yh", 1)
    out = pl.pallas_call(
        place_kernel,
        out_shape=shape((DEPTH, 64, 512)),
        in_specs=[pl.BlockSpec(memory_space=pltpu.SMEM)] + whole(4),
        out_specs=whole(1)[0],
        compiler_params=params(),
        cost_estimate=COST,
        name="place",
    )(place, order, near, far, both_cores(near, far))
    return out.reshape(DEPTH, 2, ROW, 512)


def after(value, *done):
    return lax.optimization_barrier((value,) + done)[0]


def body(inputs, preact, cotangent, weight1, weight2):
    place = jnp.stack([lax.axis_index(a) for a in AF + ("z",)]).astype(jnp.int32)
    factor = 1.0 / jnp.sqrt(F32(32 * CELLS))
    planes_first = lambda value: value.transpose(1, 0, 2)
    zero = jnp.zeros((), BF16)
    gather_inputs = lambda value: [value] + [from_ahead(value, "x", d) for d in (1, 2, 3)]

    order = make_orders(place)
    cot = planes_first(cotangent)
    far_cot = from_ahead(cot, "yh", 1)
    low, high = halo(cot[DEPTH - 1 :], cot[:1])
    rims = jnp.concatenate([low, high])
    pre = planes_first(preact)
    sources = gather_inputs(jnp.concatenate([jnp.maximum(pre, zero), planes_first(inputs)]))
    own2, core2, far2 = regroup(weight2, order)
    far2 = from_ahead(after(far2, low, high, far_cot), "yh", 1)
    far_rims = from_ahead(rims, "yh", 1)
    cot, far_cot = jnp.concatenate([cot, rims]), jnp.concatenate([far_cot, far_rims])
    grads2 = cot, far_cot, both_cores(cot, far_cot)
    weights2 = own2, far2, both_cores(core2, far2[1])
    own1, core1, far1 = regroup(weight1, after(order, low))

    unit_parts = data_by_channel(grads2, after(weights2, own1))
    far1 = from_ahead(after(far1, unit_parts[0]), "yh", 1)
    whole_filter = shape((4, 2, SRC * TAPS * 4, 3 * WIDE))
    filter2_parts = filter_sums(
        second_filter_kernel, whole_filter, after(place, unit_parts[0]), *grads2, *sources
    )
    blocks = after(moved_ahead(unit_parts, "x"), filter2_parts)
    grad = jnp.where(pre > 0, total_of(blocks), 0.0).astype(BF16)
    grad = after(grad, far1)
    far_grad = from_ahead(grad, "yh", 1)
    low, high = halo(grad[DEPTH - 1 :], grad[:1])
    rims = jnp.concatenate([low, high])
    far_rims = from_ahead(rims, "yh", 1)
    filter2_got = lax.all_to_all(after(filter2_parts, far_grad), "z", 0, 0)
    weights1 = own1, far1, both_cores(after(core1, low), far1[1])
    grad, far_grad = jnp.concatenate([grad, rims]), jnp.concatenate([far_grad, far_rims])
    grads1 = grad, far_grad, both_cores(grad, far_grad)
    filter1_parts = filter_sums(
        first_filter_kernel, (shape(whole_filter.shape[1:]),) * 4, place, *grads1, *sources
    )
    image_parts = data_by_row(after(place, filter1_parts), grads1, weights1)
    filter1_got = after(moved_ahead(filter1_parts, "z"), image_parts[0])
    sums = [total_of(list(got)).astype(BF16) for got in (filter1_got, filter2_got)]
    sums = sum_yl(jnp.stack(sums, axis=1))
    blocks = after(moved_ahead(image_parts, "x"), sums)
    input_grad = finish_image(total_of(blocks).astype(BF16), place, order)
    filter1_grad, filter2_grad = finish_filters(order, sums, factor)
    return input_grad, filter1_grad, filter2_grad


def solution(mesh):
    fine = Mesh(mesh.devices.reshape(2, 4, 2, 4, 2), AF + GZ)
    placed = (
        P(AF, GZ, None),
        P(AF, GZ, None),
        P(AF, GZ, None),
        P(None, None, None, AF, None),
        P(None, None, None, AF, None),
    )
    return jax.shard_map(
        body,
        mesh=fine,
        in_specs=placed,
        out_specs=(
            P(GZ, AF, None, None),
            P(None, None, None, AF + GZ, None),
            P(None, None, None, AF + GZ, None),
        ),
        check_vma=False,
    )
```

```python
import functools

import jax
import jax.numpy as jnp
from jax import lax
from jax.experimental import pallas as pl
from jax.experimental.pallas import tpu as pltpu
from jax.sharding import Mesh
from jax.sharding import PartitionSpec as P

AF = ("yh", "x", "core")
GZ = ("z", "yl")
SIZE = {"yh": 2, "x": 4, "core": 2, "z": 4, "yl": 2}
ROW = 32
CELLS = 1024
TAPS = 9
BLOCK = 32
WIDE = 128
DEPTH = 4
SRC = 4
DEEP = TAPS * BLOCK
K = SRC * DEEP
VMEM_BYTES = 12 * 1024 * 1024
NN = (((1,), (0,)), ((), ()))
NT = (((1,), (1,)), ((), ()))
COST = pl.CostEstimate(flops=1000, bytes_accessed=1000, transcendentals=0)
F32 = jnp.float32
BF16 = jnp.bfloat16


def params():
    return pltpu.CompilerParams(vmem_limit_bytes=VMEM_BYTES)


def whole(count):
    return [pl.BlockSpec(memory_space=pltpu.VMEM)] * count


def from_ahead(value, axis, step):
    n = SIZE[axis]
    return lax.ppermute(value, axis, [(i, (i - step) % n) for i in range(n)])


def shape(dims, kind=BF16):
    return jax.ShapeDtypeStruct(dims, kind)


def picks(place_ref, dyh, dcore):
    yh, x, core = place_ref[0], place_ref[1], place_ref[2]
    row = lax.broadcasted_iota(jnp.int32, (WIDE, 512), 0)
    lane = lax.broadcasted_iota(jnp.int32, (WIDE, 512), 1)
    column = (row // BLOCK + x) % 4
    channel = (yh + dyh) % 2 * 256 + (core + dcore) % 2 * BLOCK + column * 64 + row % BLOCK
    return jnp.where(channel == lane, 1.0, 0.0).astype(BF16)


def orders_kernel(place_ref, out_ref):
    for src in range(SRC):
        out_ref[src * WIDE : (src + 1) * WIDE, :] = picks(place_ref, src // 2, src % 2)


def make_orders(place):
    return pl.pallas_call(
        orders_kernel,
        out_shape=shape((512, 512)),
        in_specs=[pl.BlockSpec(memory_space=pltpu.SMEM)],
        out_specs=whole(1)[0],
        compiler_params=params(),
        cost_estimate=COST,
        name="orders",
    )(place)


def regroup_kernel(w_ref, order_ref, own_ref, core_ref, far_ref):
    rows = w_ref[...]
    for block, target in enumerate((own_ref, core_ref, far_ref.at[0], far_ref.at[1])):
        order = order_ref[block * WIDE : (block + 1) * WIDE, :]
        picked = lax.dot_general(rows, order, NT, preferred_element_type=F32)
        target[...] = picked.astype(BF16)


def regroup(weight, order):
    rows = weight.reshape(27 * BLOCK, 512)
    one = shape((27 * BLOCK, WIDE))
    return pl.pallas_call(
        regroup_kernel,
        out_shape=(one, one, shape((2, 27 * BLOCK, WIDE))),
        in_specs=whole(2),
        out_specs=tuple(whole(3)),
        compiler_params=params(),
        cost_estimate=COST,
        name="regroup",
    )(rows, order)


def masks():
    lane = lax.broadcasted_iota(jnp.int32, (BLOCK, CELLS), 1)
    col = lane & (ROW - 1)
    one = lambda keep: jnp.where(keep, 1.0, 0.0).astype(BF16)
    return (
        one(col < ROW - 1),
        one(col > 0),
        one(lane < CELLS - ROW),
        one(lane >= ROW),
    )


def shift_plane(refs, shifted, keep):
    left, right, top, bottom = keep
    for src, ref in enumerate(refs):
        mid = ref[...]
        across = (
            pltpu.roll(mid, CELLS - 1, 1) * left,
            mid,
            pltpu.roll(mid, 1, 1) * right,
        )
        for kx in range(3):
            rows = (
                pltpu.roll(across[kx], CELLS - ROW, 1) * top,
                across[kx],
                pltpu.roll(across[kx], ROW, 1) * bottom,
            )
            for ky in range(3):
                at = src * DEEP + (ky * 3 + kx) * BLOCK
                shifted[at : at + BLOCK, :] = rows[ky]


def plane_refs(grads, plane):
    own, rims = grads[:SRC], grads[SRC:]
    if 1 <= plane <= DEPTH:
        return [ref.at[plane - 1] for ref in own]
    return [ref.at[0 if plane == 0 else 1] for ref in rims]


def taps_of(plane):
    return max(0, 2 - plane), min(3, DEPTH + 2 - plane)


def data_sums(grads, weights, turned, shifted, total):
    own, core, far, got = weights
    for kz in range(3):
        rows = slice(kz * DEEP, (kz + 1) * DEEP)
        for src, block in enumerate((own[rows], core[rows], far[0, rows], got[1, rows])):
            shifted[0, src * DEEP : (src + 1) * DEEP, :WIDE] = block
        turned[kz * WIDE : (kz + 1) * WIDE, :] = shifted[0, :, :WIDE].T
    keep = masks()
    for plane in range(DEPTH + 2):
        slot = shifted.at[plane % 2]
        shift_plane(plane_refs(grads, plane), slot, keep)
        low, high = taps_of(plane)
        for part in range(4):
            lanes = slice(part * 256, (part + 1) * 256)
            part = lax.dot_general(
                turned[low * WIDE : high * WIDE, :], slot[:, lanes], NN, preferred_element_type=F32
            )
            for kz in range(low, high):
                at = (plane - 2 + kz) * WIDE
                piece = part[(kz - low) * WIDE : (kz - low + 1) * WIDE]
                if kz < 2:
                    piece = piece + total[at : at + WIDE, lanes]
                total[at : at + WIDE, lanes] = piece


def data_by_channel_kernel(*refs):
    grads, weights, outs = refs[:8], refs[8:12], refs[12:16]
    total = refs[-1]
    data_sums(grads, weights, *refs[16:])
    for dx in range(4):

        @pl.loop(0, DEPTH)
        def _(plane):
            at = pl.multiple_of(plane * WIDE + dx * BLOCK, BLOCK)
            outs[dx][plane] = total[pl.ds(at, BLOCK), :].astype(BF16)


def data_by_row_kernel(place_ref, *refs):
    grads, weights, outs = refs[:8], refs[8:12], refs[12:16]
    total = refs[-1]
    data_sums(grads, weights, *refs[16:])
    yh, x = place_ref[0], place_ref[1]
    for dx in range(4):
        for dyh in range(2):
            chunk = (yh + dyh) % 2 * 4 + (x + dx) % 4
            lanes = pl.ds(pl.multiple_of(chunk * WIDE, WIDE), WIDE)
            for plane in range(DEPTH):
                for block in range(4):
                    at = plane * WIDE + (dx + block) % 4 * BLOCK
                    rows = slice(block * BLOCK, (block + 1) * BLOCK)
                    outs[dx][dyh, plane, rows] = total[at : at + BLOCK, lanes].astype(BF16)


DATA_SCRATCH = [
    pltpu.VMEM((3 * WIDE, K), BF16),
    pltpu.VMEM((2, K, CELLS), BF16),
    pltpu.VMEM((DEPTH * WIDE, CELLS), F32),
]


def data_by_channel(grads, weights):
    return pl.pallas_call(
        data_by_channel_kernel,
        out_shape=(shape((DEPTH, BLOCK, CELLS)),) * 4,
        in_specs=whole(12),
        out_specs=tuple(whole(4)),
        scratch_shapes=DATA_SCRATCH,
        compiler_params=params(),
        cost_estimate=COST,
        name="data_by_channel",
    )(*grads, *weights)


def data_by_row(place, grads, weights):
    return pl.pallas_call(
        data_by_row_kernel,
        out_shape=(shape((2, DEPTH, WIDE, WIDE)),) * 4,
        in_specs=[pl.BlockSpec(memory_space=pltpu.SMEM)] + whole(12),
        out_specs=tuple(whole(4)),
        scratch_shapes=DATA_SCRATCH,
        compiler_params=params(),
        cost_estimate=COST,
        name="data_by_row",
    )(place, *grads, *weights)


def add_products(total, slot, sources, low, high, fresh):
    for src in range(SRC):
        part = lax.dot_general(
            slot[src * DEEP : (src + 1) * DEEP, :], sources, NT, preferred_element_type=F32
        )
        for kz in range(low, high):
            piece = part[:, (kz - low) * WIDE : (kz - low + 1) * WIDE]
            lanes = slice(kz * WIDE, (kz + 1) * WIDE)
            piece = piece.reshape(TAPS, 4, 8, WIDE)
            rows = slice(src * TAPS, (src + 1) * TAPS)
            if not fresh(kz):
                piece = piece + total[rows, :, :, lanes]
            total[rows, :, :, lanes] = piece


def filter_total(grads, sources, first_plane, stacked, shifted, total):
    for dx in range(4):
        for plane in range(DEPTH):
            at = plane * WIDE + dx * BLOCK
            stacked[at : at + BLOCK, :] = sources[dx][first_plane + plane]
    keep = masks()
    for plane in range(DEPTH + 2):
        slot = shifted.at[plane % 2]
        shift_plane(plane_refs(grads, plane), slot, keep)
        low, high = taps_of(plane)
        first = plane - 2 + low
        rows = stacked[first * WIDE : (first + high - low) * WIDE, :]
        add_products(total, slot, rows, low, high, lambda kz: plane == 2 - kz)


def second_filter_kernel(place_ref, *refs):
    filter_total(refs[:8], refs[8:12], 0, *refs[13:])
    for z in range(4):
        low, high = rows_of(refs[-1], z)
        refs[12][z, 0], refs[12][z, 1] = low, high


def first_filter_kernel(place_ref, *refs):
    filter_total(refs[:8], refs[8:12], DEPTH, *refs[16:])
    for dz in range(4):
        low, high = rows_of(refs[-1], (place_ref[3] + dz) % 4)
        refs[12 + dz][0], refs[12 + dz][1] = low, high


def rows_of(total, z):
    upper = lax.broadcasted_iota(jnp.int32, (18, 8, 3 * WIDE), 1) < 4
    rows = total[:, pl.ds(z, 1), :, :].reshape(18, 2, 8, 3 * WIDE)
    one, two = rows[:, 0], rows[:, 1]
    low = jnp.where(upper, one, pltpu.roll(two, 4, 1))
    high = jnp.where(upper, pltpu.roll(one, 4, 1), two)
    return [half.reshape(18 * 8, 3 * WIDE).astype(BF16) for half in (low, high)]


def filter_sums(kernel, out_shape, *args):
    return pl.pallas_call(
        kernel,
        out_shape=out_shape,
        in_specs=[pl.BlockSpec(memory_space=pltpu.SMEM)] + whole(len(args) - 1),
        out_specs=jax.tree.map(lambda _: whole(1)[0], out_shape),
        scratch_shapes=[
            pltpu.VMEM((DEPTH * WIDE, CELLS), BF16),
            pltpu.VMEM((2, K, CELLS), BF16),
            pltpu.VMEM((SRC * TAPS, 4, 8, 3 * WIDE), F32),
        ],
        compiler_params=params(),
        cost_estimate=COST,
        name="filter_sums",
    )(*args)


def both_cores(near, far):
    return from_ahead(jnp.stack([near, far]), "core", 1)


def blocks_of(near, far):
    return near, from_ahead(near, "core", 1), far, from_ahead(far, "core", 1)


def blocks_of2(own, core, far):
    return own, from_ahead(core, "core", 1), far, from_ahead(far, "core", 1)


def moved_ahead(blocks, axis):
    return [blocks[0]] + [from_ahead(blocks[d], axis, -d) for d in range(1, 4)]


def total_of(blocks):
    return sum(block.astype(F32) for block in blocks)


def halo(last, first):
    low = lax.ppermute(last, GZ, [(i, i + 1) for i in range(7)])
    high = lax.ppermute(first, GZ, [(i + 1, i) for i in range(7)])
    return low, high


def sum_yl(part):
    yl = lax.axis_index("yl")
    mine = lax.dynamic_index_in_dim(part, yl, 0, keepdims=False)
    other = lax.dynamic_index_in_dim(part, 1 - yl, 0, keepdims=False)
    return total_of([mine, from_ahead(other, "yl", 1)]).astype(BF16)


def place_filters_kernel(factor_ref, order_ref, own_ref, far_ref, got_ref, first_ref, second_ref):
    orders = [order_ref[src * WIDE : (src + 1) * WIDE, :] for src in range(SRC)]
    for index, out_ref in enumerate((first_ref, second_ref)):
        for kz in range(3):
            lanes = slice(kz * WIDE, (kz + 1) * WIDE)
            total = None
            for order, rows in zip(
                orders,
                (own_ref[index, :, lanes], got_ref[0, index, :, lanes], far_ref[index, :, lanes], got_ref[1, index, :, lanes]),
            ):
                part = lax.dot_general(rows, order, NN, preferred_element_type=F32)
                total = part if total is None else total + part
            total = total * factor_ref[0]
            for tap in range(TAPS):
                out_ref[kz * TAPS + tap] = total[tap * 4 : (tap + 1) * 4]


def finish_filters(order, sums, factor):
    rows = sums.reshape(2, 2, 2, TAPS * 4, 3 * WIDE).transpose(1, 2, 0, 3, 4)
    far = from_ahead(rows[1], "yh", 1)
    got = both_cores(rows[0, 1], far[1])
    outs = pl.pallas_call(
        place_filters_kernel,
        out_shape=(shape((27, 4, 512), F32),) * 2,
        in_specs=[pl.BlockSpec(memory_space=pltpu.SMEM)] + whole(4),
        out_specs=tuple(whole(2)),
        compiler_params=params(),
        cost_estimate=COST,
        name="place_filters",
    )(factor.reshape(1), order, rows[0, 0], far[0], got)
    return [out.reshape(3, 3, 3, 4, 512) for out in outs]


def place_kernel(place_ref, order_ref, own_ref, far_ref, got_ref, out_ref):
    upper = place_ref[2] == 1
    blocks = own_ref, got_ref.at[0], far_ref, got_ref.at[1]
    for pair in range(DEPTH // 2):
        halves = []
        for plane in (2 * pair, 2 * pair + 1):
            rows = jnp.concatenate([ref[plane] for ref in blocks], axis=0)
            halves.append(jnp.where(upper, rows[:, 64:], rows[:, :64]))
        cells = jnp.concatenate(halves, axis=1).T
        part = lax.dot_general(cells, order_ref[...], NN, preferred_element_type=F32).astype(BF16)
        out_ref[2 * pair], out_ref[2 * pair + 1] = part[:64], part[64:]


def finish_image(part, place, order):
    near = part[0]
    far = from_ahead(part[1], "yh", 1)
    out = pl.pallas_call(
        place_kernel,
        out_shape=shape((DEPTH, 64, 512)),
        in_specs=[pl.BlockSpec(memory_space=pltpu.SMEM)] + whole(4),
        out_specs=whole(1)[0],
        compiler_params=params(),
        cost_estimate=COST,
        name="place",
    )(place, order, near, far, both_cores(near, far))
    return out.reshape(DEPTH, 2, ROW, 512)


def after(value, *done):
    return lax.optimization_barrier((value,) + done)[0]


def body(inputs, preact, cotangent, weight1, weight2):
    place = jnp.stack([lax.axis_index(a) for a in AF + ("z",)]).astype(jnp.int32)
    factor = 1.0 / jnp.sqrt(F32(32 * CELLS))
    planes_first = lambda value: value.transpose(1, 0, 2)
    zero = jnp.zeros((), BF16)
    gather_inputs = lambda value: [value] + [from_ahead(value, "x", d) for d in (1, 2, 3)]

    order = make_orders(place)
    pre = planes_first(preact)
    source = jnp.concatenate([jnp.maximum(pre, zero), planes_first(inputs)])
    ahead, behind = from_ahead(source, "x", 1), from_ahead(source, "x", 3)
    cot = planes_first(cotangent)
    far_cot = from_ahead(cot, "yh", 1)
    low, high = halo(cot[DEPTH - 1 :], cot[:1])
    rims = jnp.concatenate([low, high])
    sources = source, ahead, from_ahead(after(source, far_cot), "x", 2), behind
    own2, core2, far2 = regroup(weight2, order)
    far2 = from_ahead(after(far2, low, high), "yh", 1)
    far_rims = from_ahead(rims, "yh", 1)
    far2, far_cot = after((far2, far_cot), far_rims, ahead, behind)
    grads2 = blocks_of(cot, far_cot) + blocks_of(rims, far_rims)
    weights2 = blocks_of2(own2, core2, far2)
    own1, core1, far1 = regroup(weight1, after(order, low))

    unit_parts = data_by_channel(grads2, after(weights2, own1, *sources))
    far1 = from_ahead(after(far1, unit_parts[0]), "yh", 1)
    one = shape((2, SRC * TAPS * 4, 3 * WIDE))
    every = shape((4,) + one.shape)
    filter2_parts = filter_sums(second_filter_kernel, every, after(place, unit_parts[0]), *grads2, *sources)
    blocks = after(moved_ahead(unit_parts, "x"), filter2_parts)
    grad = jnp.where(pre > 0, total_of(blocks), 0.0).astype(BF16)
    grad = after(grad, far1)
    low, high = halo(grad[DEPTH - 1 :], grad[:1])
    far_grad = from_ahead(grad, "yh", 1)
    rims = jnp.concatenate([low, high])
    far_rims = from_ahead(rims, "yh", 1)
    filter2_got = lax.all_to_all(filter2_parts, "z", 0, 0)
    weights1 = blocks_of2(own1, core1, after(far1, low))
    grads1 = blocks_of(grad, far_grad) + blocks_of(rims, far_rims)
    filter_parts = filter_sums(first_filter_kernel, (one,) * 4, place, *grads1, *sources)
    image_parts = data_by_row(after(place, filter_parts[0]), grads1, weights1)
    filter1_got = after(moved_ahead(filter_parts, "z"), image_parts[0])
    sums = [total_of(list(got)).astype(BF16) for got in (filter1_got, filter2_got)]
    sums = sum_yl(jnp.stack(sums, axis=1))
    blocks = after(moved_ahead(image_parts, "x"), sums)
    input_grad = finish_image(total_of(blocks).astype(BF16), place, order)
    filter1_grad, filter2_grad = finish_filters(order, sums, factor)
    return input_grad, filter1_grad, filter2_grad


def solution(mesh):
    fine = Mesh(mesh.devices.reshape(2, 4, 2, 4, 2), AF + GZ)
    placed = (
        P(AF, GZ, None),
        P(AF, GZ, None),
        P(AF, GZ, None),
        P(None, None, None, AF, None),
        P(None, None, None, AF, None),
    )
    return jax.shard_map(
        body,
        mesh=fine,
        in_specs=placed,
        out_specs=(
            P(GZ, AF, None, None),
            P(None, None, None, AF + GZ, None),
            P(None, None, None, AF + GZ, None),
        ),
        check_vma=False,
    )
```

```python
import functools

import jax
import jax.numpy as jnp
from jax import lax
from jax.experimental import pallas as pl
from jax.experimental.pallas import tpu as pltpu
from jax.sharding import Mesh
from jax.sharding import PartitionSpec as P

AF = ("yh", "x", "core")
GZ = ("z", "yl")
SIZE = {"yh": 2, "x": 4, "core": 2, "z": 4, "yl": 2}
ROW = 32
CELLS = 1024
TAPS = 9
BLOCK = 32
WIDE = 128
DEPTH = 4
SRC = 4
DEEP = TAPS * BLOCK
K = SRC * DEEP
VMEM_BYTES = 12 * 1024 * 1024
NN = (((1,), (0,)), ((), ()))
NT = (((1,), (1,)), ((), ()))
COST = pl.CostEstimate(flops=1000, bytes_accessed=1000, transcendentals=0)
F32 = jnp.float32
BF16 = jnp.bfloat16


def params():
    return pltpu.CompilerParams(vmem_limit_bytes=VMEM_BYTES)


def whole(count):
    return [pl.BlockSpec(memory_space=pltpu.VMEM)] * count


def from_ahead(value, axis, step):
    n = SIZE[axis]
    return lax.ppermute(value, axis, [(i, (i - step) % n) for i in range(n)])


def shape(dims, kind=BF16):
    return jax.ShapeDtypeStruct(dims, kind)


def picks(place_ref, dyh, dcore):
    yh, x, core = place_ref[0], place_ref[1], place_ref[2]
    row = lax.broadcasted_iota(jnp.int32, (WIDE, 512), 0)
    lane = lax.broadcasted_iota(jnp.int32, (WIDE, 512), 1)
    column = (row // BLOCK + x) % 4
    channel = (yh + dyh) % 2 * 256 + (core + dcore) % 2 * BLOCK + column * 64 + row % BLOCK
    return jnp.where(channel == lane, 1.0, 0.0).astype(BF16)


def orders_kernel(place_ref, out_ref):
    for src in range(SRC):
        out_ref[src * WIDE : (src + 1) * WIDE, :] = picks(place_ref, src // 2, src % 2)


def make_orders(place):
    return pl.pallas_call(
        orders_kernel,
        out_shape=shape((512, 512)),
        in_specs=[pl.BlockSpec(memory_space=pltpu.SMEM)],
        out_specs=whole(1)[0],
        compiler_params=params(),
        cost_estimate=COST,
        name="orders",
    )(place)


def regroup_kernel(w_ref, order_ref, own_ref, core_ref, far_ref):
    rows = w_ref[...]
    for block, target in enumerate((own_ref, core_ref, far_ref.at[0], far_ref.at[1])):
        order = order_ref[block * WIDE : (block + 1) * WIDE, :]
        picked = lax.dot_general(rows, order, NT, preferred_element_type=F32)
        target[...] = picked.astype(BF16)


def regroup(weight, order):
    rows = weight.reshape(27 * BLOCK, 512)
    one = shape((27 * BLOCK, WIDE))
    return pl.pallas_call(
        regroup_kernel,
        out_shape=(one, one, shape((2, 27 * BLOCK, WIDE))),
        in_specs=whole(2),
        out_specs=tuple(whole(3)),
        compiler_params=params(),
        cost_estimate=COST,
        name="regroup",
    )(rows, order)


def masks():
    lane = lax.broadcasted_iota(jnp.int32, (BLOCK, CELLS), 1)
    col = lane & (ROW - 1)
    one = lambda keep: jnp.where(keep, 1.0, 0.0).astype(BF16)
    return (
        one(col < ROW - 1),
        one(col > 0),
        one(lane < CELLS - ROW),
        one(lane >= ROW),
    )


def shift_plane(refs, shifted, keep):
    left, right, top, bottom = keep
    for src, ref in enumerate(refs):
        mid = ref[...]
        across = (
            pltpu.roll(mid, CELLS - 1, 1) * left,
            mid,
            pltpu.roll(mid, 1, 1) * right,
        )
        for kx in range(3):
            rows = (
                pltpu.roll(across[kx], CELLS - ROW, 1) * top,
                across[kx],
                pltpu.roll(across[kx], ROW, 1) * bottom,
            )
            for ky in range(3):
                at = src * DEEP + (ky * 3 + kx) * BLOCK
                shifted[at : at + BLOCK, :] = rows[ky]


def plane_refs(grads, plane):
    own, rims = grads[:SRC], grads[SRC:]
    if 1 <= plane <= DEPTH:
        return [ref.at[plane - 1] for ref in own]
    return [ref.at[0 if plane == 0 else 1] for ref in rims]


def taps_of(plane):
    return max(0, 2 - plane), min(3, DEPTH + 2 - plane)


def data_sums(grads, weights, turned, shifted, total):
    own, core, far, got = weights
    for kz in range(3):
        rows = slice(kz * DEEP, (kz + 1) * DEEP)
        for src, block in enumerate((own[rows], core[rows], far[0, rows], got[1, rows])):
            shifted[0, src * DEEP : (src + 1) * DEEP, :WIDE] = block
        turned[kz * WIDE : (kz + 1) * WIDE, :] = shifted[0, :, :WIDE].T
    keep = masks()
    for plane in range(DEPTH + 2):
        slot = shifted.at[plane % 2]
        shift_plane(plane_refs(grads, plane), slot, keep)
        low, high = taps_of(plane)
        for part in range(4):
            lanes = slice(part * 256, (part + 1) * 256)
            part = lax.dot_general(
                turned[low * WIDE : high * WIDE, :], slot[:, lanes], NN, preferred_element_type=F32
            )
            for kz in range(low, high):
                at = (plane - 2 + kz) * WIDE
                piece = part[(kz - low) * WIDE : (kz - low + 1) * WIDE]
                if kz < 2:
                    piece = piece + total[at : at + WIDE, lanes]
                total[at : at + WIDE, lanes] = piece


def data_by_channel_kernel(*refs):
    grads, weights, outs = refs[:8], refs[8:12], refs[12:16]
    total = refs[-1]
    data_sums(grads, weights, *refs[16:])
    for dx in range(4):

        @pl.loop(0, DEPTH)
        def _(plane):
            at = pl.multiple_of(plane * WIDE + dx * BLOCK, BLOCK)
            outs[dx][plane] = total[pl.ds(at, BLOCK), :].astype(BF16)


def data_by_row_kernel(place_ref, *refs):
    grads, weights, outs = refs[:8], refs[8:12], refs[12:16]
    total = refs[-1]
    data_sums(grads, weights, *refs[16:])
    yh, x = place_ref[0], place_ref[1]
    for dx in range(4):
        for dyh in range(2):
            chunk = (yh + dyh) % 2 * 4 + (x + dx) % 4
            lanes = pl.ds(pl.multiple_of(chunk * WIDE, WIDE), WIDE)
            for plane in range(DEPTH):
                for block in range(4):
                    at = plane * WIDE + (dx + block) % 4 * BLOCK
                    rows = slice(block * BLOCK, (block + 1) * BLOCK)
                    outs[dx][dyh, plane, rows] = total[at : at + BLOCK, lanes].astype(BF16)


DATA_SCRATCH = [
    pltpu.VMEM((3 * WIDE, K), BF16),
    pltpu.VMEM((2, K, CELLS), BF16),
    pltpu.VMEM((DEPTH * WIDE, CELLS), F32),
]


def data_by_channel(grads, weights):
    return pl.pallas_call(
        data_by_channel_kernel,
        out_shape=(shape((DEPTH, BLOCK, CELLS)),) * 4,
        in_specs=whole(12),
        out_specs=tuple(whole(4)),
        scratch_shapes=DATA_SCRATCH,
        compiler_params=params(),
        cost_estimate=COST,
        name="data_by_channel",
    )(*grads, *weights)


def data_by_row(place, grads, weights):
    return pl.pallas_call(
        data_by_row_kernel,
        out_shape=(shape((2, DEPTH, WIDE, WIDE)),) * 4,
        in_specs=[pl.BlockSpec(memory_space=pltpu.SMEM)] + whole(12),
        out_specs=tuple(whole(4)),
        scratch_shapes=DATA_SCRATCH,
        compiler_params=params(),
        cost_estimate=COST,
        name="data_by_row",
    )(place, *grads, *weights)


def add_products(total, slot, sources, low, high, fresh):
    for src in range(SRC):
        part = lax.dot_general(
            slot[src * DEEP : (src + 1) * DEEP, :], sources, NT, preferred_element_type=F32
        )
        for kz in range(low, high):
            piece = part[:, (kz - low) * WIDE : (kz - low + 1) * WIDE]
            lanes = slice(kz * WIDE, (kz + 1) * WIDE)
            piece = piece.reshape(TAPS, 4, 8, WIDE)
            rows = slice(src * TAPS, (src + 1) * TAPS)
            if not fresh(kz):
                piece = piece + total[rows, :, :, lanes]
            total[rows, :, :, lanes] = piece


def filter_total(grads, sources, first_plane, stacked, shifted, total):
    for dx in range(4):
        for plane in range(DEPTH):
            at = plane * WIDE + dx * BLOCK
            stacked[at : at + BLOCK, :] = sources[dx][first_plane + plane]
    keep = masks()
    for plane in range(DEPTH + 2):
        slot = shifted.at[plane % 2]
        shift_plane(plane_refs(grads, plane), slot, keep)
        low, high = taps_of(plane)
        first = plane - 2 + low
        rows = stacked[first * WIDE : (first + high - low) * WIDE, :]
        add_products(total, slot, rows, low, high, lambda kz: plane == 2 - kz)


def second_filter_kernel(place_ref, *refs):
    filter_total(refs[:8], refs[8:12], 0, *refs[13:])
    for z in range(4):
        low, high = rows_of(refs[-1], z)
        refs[12][z, 0], refs[12][z, 1] = low, high


def first_filter_kernel(place_ref, *refs):
    filter_total(refs[:8], refs[8:12], DEPTH, *refs[18:])
    for dz in range(4):
        low, high = rows_of(refs[-1], (place_ref[3] + dz) % 4)
        refs[13 + dz][0], refs[13 + dz][1] = low, high
    got_ref, sum_ref = refs[12], refs[17]
    for yl in range(2):
        sum_ref[yl] = total_of([got_ref[z, yl] for z in range(4)]).astype(BF16)


def z_sum_kernel(place_ref, own_ref, a_ref, b_ref, c_ref, second_ref, mine_ref, other_ref):
    yl = place_ref[4]
    for at, out_ref in ((yl, mine_ref), (1 - yl, other_ref)):
        out_ref[0] = total_of([ref[at] for ref in (own_ref, a_ref, b_ref, c_ref)]).astype(BF16)
        out_ref[1] = second_ref[at]


def rows_of(total, z):
    upper = lax.broadcasted_iota(jnp.int32, (18, 8, 3 * WIDE), 1) < 4
    rows = total[:, pl.ds(z, 1), :, :].reshape(18, 2, 8, 3 * WIDE)
    one, two = rows[:, 0], rows[:, 1]
    low = jnp.where(upper, one, pltpu.roll(two, 4, 1))
    high = jnp.where(upper, pltpu.roll(one, 4, 1), two)
    return [half.reshape(18 * 8, 3 * WIDE).astype(BF16) for half in (low, high)]


def filter_sums(kernel, out_shape, *args):
    return pl.pallas_call(
        kernel,
        out_shape=out_shape,
        in_specs=[pl.BlockSpec(memory_space=pltpu.SMEM)] + whole(len(args) - 1),
        out_specs=jax.tree.map(lambda _: whole(1)[0], out_shape),
        scratch_shapes=[
            pltpu.VMEM((DEPTH * WIDE, CELLS), BF16),
            pltpu.VMEM((2, K, CELLS), BF16),
            pltpu.VMEM((SRC * TAPS, 4, 8, 3 * WIDE), F32),
        ],
        compiler_params=params(),
        cost_estimate=COST,
        name="filter_sums",
    )(*args)


def both_cores(near, far):
    return from_ahead(jnp.stack([near, far]), "core", 1)


def blocks_of(near, far):
    return near, from_ahead(near, "core", 1), far, from_ahead(far, "core", 1)


def blocks_of2(own, core, far):
    return own, from_ahead(core, "core", 1), far, from_ahead(far, "core", 1)


def moved_ahead(blocks, axis):
    return [blocks[0]] + [from_ahead(blocks[d], axis, -d) for d in range(1, 4)]


def total_of(blocks):
    return sum(block.astype(F32) for block in blocks)


def halo(last, first):
    low = lax.ppermute(last, GZ, [(i, i + 1) for i in range(7)])
    high = lax.ppermute(first, GZ, [(i + 1, i) for i in range(7)])
    return low, high


def sum_gz(place, blocks, second):
    part = shape((2, SRC * TAPS * 4, 3 * WIDE))
    mine, other = pl.pallas_call(
        z_sum_kernel,
        out_shape=(part, part),
        in_specs=[pl.BlockSpec(memory_space=pltpu.SMEM)] + whole(5),
        out_specs=tuple(whole(2)),
        compiler_params=params(),
        cost_estimate=COST,
        name="z_sum",
    )(place, *blocks, second)
    return total_of([mine, from_ahead(other, "yl", 1)]).astype(BF16)


def place_filters_kernel(factor_ref, order_ref, own_ref, far_ref, got_ref, first_ref, second_ref):
    orders = [order_ref[src * WIDE : (src + 1) * WIDE, :] for src in range(SRC)]
    for index, out_ref in enumerate((first_ref, second_ref)):
        for kz in range(3):
            lanes = slice(kz * WIDE, (kz + 1) * WIDE)
            total = None
            for order, rows in zip(
                orders,
                (own_ref[index, :, lanes], got_ref[0, index, :, lanes], far_ref[index, :, lanes], got_ref[1, index, :, lanes]),
            ):
                part = lax.dot_general(rows, order, NN, preferred_element_type=F32)
                total = part if total is None else total + part
            total = total * factor_ref[0]
            for tap in range(TAPS):
                out_ref[kz * TAPS + tap] = total[tap * 4 : (tap + 1) * 4]


def near_and_far(sums):
    rows = sums.reshape(2, 2, 2, TAPS * 4, 3 * WIDE).transpose(1, 2, 0, 3, 4)
    return rows, from_ahead(rows[1], "yh", 1)


def finish_filters(order, rows, far, factor):
    got = both_cores(rows[0, 1], far[1])
    outs = pl.pallas_call(
        place_filters_kernel,
        out_shape=(shape((27, 4, 512), F32),) * 2,
        in_specs=[pl.BlockSpec(memory_space=pltpu.SMEM)] + whole(4),
        out_specs=tuple(whole(2)),
        compiler_params=params(),
        cost_estimate=COST,
        name="place_filters",
    )(factor.reshape(1), order, rows[0, 0], far[0], got)
    return [out.reshape(3, 3, 3, 4, 512) for out in outs]


def place_kernel(place_ref, order_ref, own_ref, far_ref, got_ref, out_ref):
    upper = place_ref[2] == 1
    blocks = own_ref, got_ref.at[0], far_ref, got_ref.at[1]
    for pair in range(DEPTH // 2):
        halves = []
        for plane in (2 * pair, 2 * pair + 1):
            rows = jnp.concatenate([ref[plane] for ref in blocks], axis=0)
            halves.append(jnp.where(upper, rows[:, 64:], rows[:, :64]))
        cells = jnp.concatenate(halves, axis=1).T
        part = lax.dot_general(cells, order_ref[...], NN, preferred_element_type=F32).astype(BF16)
        out_ref[2 * pair], out_ref[2 * pair + 1] = part[:64], part[64:]


def finish_image(part, place, order, done):
    near = part[0]
    far = after(from_ahead(part[1], "yh", 1), done)
    out = pl.pallas_call(
        place_kernel,
        out_shape=shape((DEPTH, 64, 512)),
        in_specs=[pl.BlockSpec(memory_space=pltpu.SMEM)] + whole(4),
        out_specs=whole(1)[0],
        compiler_params=params(),
        cost_estimate=COST,
        name="place",
    )(place, order, near, far, both_cores(near, far))
    return out.reshape(DEPTH, 2, ROW, 512)


def after(value, *done):
    return lax.optimization_barrier((value,) + done)[0]


def body(inputs, preact, cotangent, weight1, weight2):
    place = jnp.stack([lax.axis_index(a) for a in AF + GZ]).astype(jnp.int32)
    factor = 1.0 / jnp.sqrt(F32(32 * CELLS))
    planes_first = lambda value: value.transpose(1, 0, 2)
    zero = jnp.zeros((), BF16)
    gather_inputs = lambda value: [value] + [from_ahead(value, "x", d) for d in (1, 2, 3)]

    order = make_orders(place)
    pre = planes_first(preact)
    source = jnp.concatenate([jnp.maximum(pre, zero), planes_first(inputs)])
    ahead, behind = from_ahead(source, "x", 1), from_ahead(source, "x", 3)
    cot = planes_first(cotangent)
    far_cot = from_ahead(cot, "yh", 1)
    low, high = halo(cot[DEPTH - 1 :], cot[:1])
    rims = jnp.concatenate([low, high])
    sources = source, ahead, from_ahead(after(source, far_cot), "x", 2), behind
    own2, core2, far2 = regroup(weight2, order)
    far2 = from_ahead(after(far2, low, high), "yh", 1)
    far_rims = from_ahead(rims, "yh", 1)
    far2, far_cot = after((far2, far_cot), far_rims, ahead, behind)
    grads2 = blocks_of(cot, far_cot) + blocks_of(rims, far_rims)
    weights2 = blocks_of2(own2, core2, far2)
    own1, core1, far1 = regroup(weight1, after(order, low))

    unit_parts = data_by_channel(grads2, after(weights2, own1, *sources))
    far1 = from_ahead(after(far1, unit_parts[0]), "yh", 1)
    one = shape((2, SRC * TAPS * 4, 3 * WIDE))
    every = shape((4,) + one.shape)
    filter2_parts = filter_sums(second_filter_kernel, every, after(place, unit_parts[0]), *grads2, *sources)
    blocks = after(moved_ahead(unit_parts, "x"), filter2_parts)
    grad = jnp.where(pre > 0, total_of(blocks), 0.0).astype(BF16)
    grad = after(grad, far1)
    low, high = halo(grad[DEPTH - 1 :], grad[:1])
    far_grad = from_ahead(grad, "yh", 1)
    rims = jnp.concatenate([low, high])
    far_rims = from_ahead(rims, "yh", 1)
    filter2_got = lax.all_to_all(filter2_parts, "z", 0, 0)
    weights1 = blocks_of2(own1, core1, after(far1, low))
    grads1 = blocks_of(grad, far_grad) + blocks_of(rims, far_rims)
    *filter_parts, filter2_sum = filter_sums(
        first_filter_kernel, (one,) * 5, place, *grads1, *sources, filter2_got
    )
    image_parts = data_by_row(after(place, filter_parts[0]), grads1, weights1)
    filter1_got = after(moved_ahead(filter_parts, "z"), image_parts[0])
    sums = sum_gz(place, filter1_got, filter2_sum)
    rows, far = near_and_far(sums)
    blocks = after(moved_ahead(image_parts, "x"), far)
    filter1_grad, filter2_grad = finish_filters(order, rows, far, factor)
    input_grad = finish_image(total_of(blocks).astype(BF16), place, order, filter1_grad)
    return input_grad, filter1_grad, filter2_grad


def solution(mesh):
    fine = Mesh(mesh.devices.reshape(2, 4, 2, 4, 2), AF + GZ)
    placed = (
        P(AF, GZ, None),
        P(AF, GZ, None),
        P(AF, GZ, None),
        P(None, None, None, AF, None),
        P(None, None, None, AF, None),
    )
    return jax.shard_map(
        body,
        mesh=fine,
        in_specs=placed,
        out_specs=(
            P(GZ, AF, None, None),
            P(None, None, None, AF + GZ, None),
            P(None, None, None, AF + GZ, None),
        ),
        check_vma=False,
    )
```

```python
import functools

import jax
import jax.numpy as jnp
from jax import lax
from jax.experimental import pallas as pl
from jax.experimental.pallas import tpu as pltpu
from jax.sharding import Mesh
from jax.sharding import PartitionSpec as P

AF = ("yh", "x", "core")
GZ = ("z", "yl")
SIZE = {"yh": 2, "x": 4, "core": 2, "z": 4, "yl": 2}
ROW = 32
CELLS = 1024
TAPS = 9
BLOCK = 32
WIDE = 128
DEPTH = 4
SRC = 4
DEEP = TAPS * BLOCK
K = SRC * DEEP
VMEM_BYTES = 12 * 1024 * 1024
NN = (((1,), (0,)), ((), ()))
NT = (((1,), (1,)), ((), ()))
COST = pl.CostEstimate(flops=1000, bytes_accessed=1000, transcendentals=0)
F32 = jnp.float32
BF16 = jnp.bfloat16


def params():
    return pltpu.CompilerParams(vmem_limit_bytes=VMEM_BYTES)


def whole(count):
    return [pl.BlockSpec(memory_space=pltpu.VMEM)] * count


def from_ahead(value, axis, step):
    n = SIZE[axis]
    return lax.ppermute(value, axis, [(i, (i - step) % n) for i in range(n)])


def shape(dims, kind=BF16):
    return jax.ShapeDtypeStruct(dims, kind)


def picks(place_ref, dyh, dcore):
    yh, x, core = place_ref[0], place_ref[1], place_ref[2]
    row = lax.broadcasted_iota(jnp.int32, (WIDE, 512), 0)
    lane = lax.broadcasted_iota(jnp.int32, (WIDE, 512), 1)
    column = (row // BLOCK + x) % 4
    channel = (yh + dyh) % 2 * 256 + (core + dcore) % 2 * BLOCK + column * 64 + row % BLOCK
    return jnp.where(channel == lane, 1.0, 0.0).astype(BF16)


def orders_kernel(place_ref, out_ref):
    for src in range(SRC):
        out_ref[src * WIDE : (src + 1) * WIDE, :] = picks(place_ref, src // 2, src % 2)


def make_orders(place):
    return pl.pallas_call(
        orders_kernel,
        out_shape=shape((512, 512)),
        in_specs=[pl.BlockSpec(memory_space=pltpu.SMEM)],
        out_specs=whole(1)[0],
        compiler_params=params(),
        cost_estimate=COST,
        name="orders",
    )(place)


def regroup_kernel(w_ref, order_ref, own_ref, core_ref, far_ref):
    rows = w_ref[...]
    for block, target in enumerate((own_ref, core_ref, far_ref.at[0], far_ref.at[1])):
        order = order_ref[block * WIDE : (block + 1) * WIDE, :]
        picked = lax.dot_general(rows, order, NT, preferred_element_type=F32)
        target[...] = picked.astype(BF16)


def regroup(weight, order):
    rows = weight.reshape(27 * BLOCK, 512)
    one = shape((27 * BLOCK, WIDE))
    return pl.pallas_call(
        regroup_kernel,
        out_shape=(one, one, shape((2, 27 * BLOCK, WIDE))),
        in_specs=whole(2),
        out_specs=tuple(whole(3)),
        compiler_params=params(),
        cost_estimate=COST,
        name="regroup",
    )(rows, order)


def masks():
    lane = lax.broadcasted_iota(jnp.int32, (BLOCK, CELLS), 1)
    col = lane & (ROW - 1)
    one = lambda keep: jnp.where(keep, 1.0, 0.0).astype(BF16)
    return (
        one(col < ROW - 1),
        one(col > 0),
        one(lane < CELLS - ROW),
        one(lane >= ROW),
    )


def shift_plane(refs, shifted, keep):
    left, right, top, bottom = keep
    for src, ref in enumerate(refs):
        mid = ref[...]
        across = (
            pltpu.roll(mid, CELLS - 1, 1) * left,
            mid,
            pltpu.roll(mid, 1, 1) * right,
        )
        for kx in range(3):
            rows = (
                pltpu.roll(across[kx], CELLS - ROW, 1) * top,
                across[kx],
                pltpu.roll(across[kx], ROW, 1) * bottom,
            )
            for ky in range(3):
                at = src * DEEP + (ky * 3 + kx) * BLOCK
                shifted[at : at + BLOCK, :] = rows[ky]


def plane_refs(grads, plane):
    own, rims = grads[:SRC], grads[SRC:]
    if 1 <= plane <= DEPTH:
        return [ref.at[plane - 1] for ref in own]
    return [ref.at[0 if plane == 0 else 1] for ref in rims]


def taps_of(plane):
    return max(0, 2 - plane), min(3, DEPTH + 2 - plane)


def data_sums(grads, weights, turned, shifted, total):
    own, core, far, got = weights
    for kz in range(3):
        rows = slice(kz * DEEP, (kz + 1) * DEEP)
        for src, block in enumerate((own[rows], core[rows], far[0, rows], got[1, rows])):
            shifted[0, src * DEEP : (src + 1) * DEEP, :WIDE] = block
        turned[kz * WIDE : (kz + 1) * WIDE, :] = shifted[0, :, :WIDE].T
    keep = masks()
    for plane in range(DEPTH + 2):
        slot = shifted.at[plane % 2]
        shift_plane(plane_refs(grads, plane), slot, keep)
        low, high = taps_of(plane)
        for part in range(4):
            lanes = slice(part * 256, (part + 1) * 256)
            part = lax.dot_general(
                turned[low * WIDE : high * WIDE, :], slot[:, lanes], NN, preferred_element_type=F32
            )
            for kz in range(low, high):
                at = (plane - 2 + kz) * WIDE
                piece = part[(kz - low) * WIDE : (kz - low + 1) * WIDE]
                if kz < 2:
                    piece = piece + total[at : at + WIDE, lanes]
                total[at : at + WIDE, lanes] = piece


def data_by_channel_kernel(*refs):
    grads, weights, outs = refs[:8], refs[8:12], refs[12:16]
    total = refs[-1]
    data_sums(grads, weights, *refs[16:])
    for dx in range(4):

        @pl.loop(0, DEPTH)
        def _(plane):
            at = pl.multiple_of(plane * WIDE + dx * BLOCK, BLOCK)
            outs[dx][plane] = total[pl.ds(at, BLOCK), :].astype(BF16)


def data_by_row_kernel(place_ref, *refs):
    grads, weights, outs = refs[:8], refs[8:12], refs[12:16]
    total = refs[-1]
    data_sums(grads, weights, *refs[16:])
    yh, x = place_ref[0], place_ref[1]
    for dx in range(4):
        for dyh in range(2):
            chunk = (yh + dyh) % 2 * 4 + (x + dx) % 4
            lanes = pl.ds(pl.multiple_of(chunk * WIDE, WIDE), WIDE)
            for plane in range(DEPTH):
                for block in range(4):
                    at = plane * WIDE + (dx + block) % 4 * BLOCK
                    rows = slice(block * BLOCK, (block + 1) * BLOCK)
                    outs[dx][dyh, plane, rows] = total[at : at + BLOCK, lanes].astype(BF16)


DATA_SCRATCH = [
    pltpu.VMEM((3 * WIDE, K), BF16),
    pltpu.VMEM((2, K, CELLS), BF16),
    pltpu.VMEM((DEPTH * WIDE, CELLS), F32),
]


def data_by_channel(grads, weights):
    return pl.pallas_call(
        data_by_channel_kernel,
        out_shape=(shape((DEPTH, BLOCK, CELLS)),) * 4,
        in_specs=whole(12),
        out_specs=tuple(whole(4)),
        scratch_shapes=DATA_SCRATCH,
        compiler_params=params(),
        cost_estimate=COST,
        name="data_by_channel",
    )(*grads, *weights)


def data_by_row(place, grads, weights):
    return pl.pallas_call(
        data_by_row_kernel,
        out_shape=(shape((2, DEPTH, WIDE, WIDE)),) * 4,
        in_specs=[pl.BlockSpec(memory_space=pltpu.SMEM)] + whole(12),
        out_specs=tuple(whole(4)),
        scratch_shapes=DATA_SCRATCH,
        compiler_params=params(),
        cost_estimate=COST,
        name="data_by_row",
    )(place, *grads, *weights)


def add_products(total, slot, sources, low, high, fresh):
    for src in range(SRC):
        part = lax.dot_general(
            slot[src * DEEP : (src + 1) * DEEP, :], sources, NT, preferred_element_type=F32
        )
        for kz in range(low, high):
            piece = part[:, (kz - low) * WIDE : (kz - low + 1) * WIDE]
            lanes = slice(kz * WIDE, (kz + 1) * WIDE)
            piece = piece.reshape(TAPS, 4, 8, WIDE)
            rows = slice(src * TAPS, (src + 1) * TAPS)
            if not fresh(kz):
                piece = piece + total[rows, :, :, lanes]
            total[rows, :, :, lanes] = piece


def filter_total(grads, sources, first_plane, stacked, shifted, total):
    for dx in range(4):
        for plane in range(DEPTH):
            at = plane * WIDE + dx * BLOCK
            stacked[at : at + BLOCK, :] = sources[dx][first_plane + plane]
    keep = masks()
    for plane in range(DEPTH + 2):
        slot = shifted.at[plane % 2]
        shift_plane(plane_refs(grads, plane), slot, keep)
        low, high = taps_of(plane)
        first = plane - 2 + low
        rows = stacked[first * WIDE : (first + high - low) * WIDE, :]
        add_products(total, slot, rows, low, high, lambda kz: plane == 2 - kz)


def second_filter_kernel(place_ref, *refs):
    filter_total(refs[:8], refs[8:12], 0, *refs[13:])
    for z in range(4):
        low, high = rows_of(refs[-1], z)
        refs[12][z, 0], refs[12][z, 1] = low, high


def first_filter_kernel(place_ref, *refs):
    filter_total(refs[:8], refs[8:12], DEPTH, *refs[18:])
    for dz in range(4):
        low, high = rows_of(refs[-1], (place_ref[3] + dz) % 4)
        refs[13 + dz][0], refs[13 + dz][1] = low, high
    got_ref, sum_ref = refs[12], refs[17]
    for yl in range(2):
        sum_ref[yl] = total_of([got_ref[z, yl] for z in range(4)]).astype(BF16)


def z_sum_kernel(place_ref, own_ref, a_ref, b_ref, c_ref, second_ref, mine_ref, other_ref):
    yl = place_ref[4]
    for at, out_ref in ((yl, mine_ref), (1 - yl, other_ref)):
        out_ref[0] = total_of([ref[at] for ref in (own_ref, a_ref, b_ref, c_ref)]).astype(BF16)
        out_ref[1] = second_ref[at]


def rows_of(total, z):
    upper = lax.broadcasted_iota(jnp.int32, (18, 8, 3 * WIDE), 1) < 4
    rows = total[:, pl.ds(z, 1), :, :].reshape(18, 2, 8, 3 * WIDE)
    one, two = rows[:, 0], rows[:, 1]
    low = jnp.where(upper, one, pltpu.roll(two, 4, 1))
    high = jnp.where(upper, pltpu.roll(one, 4, 1), two)
    return [half.reshape(18 * 8, 3 * WIDE).astype(BF16) for half in (low, high)]


def filter_sums(kernel, out_shape, *args):
    return pl.pallas_call(
        kernel,
        out_shape=out_shape,
        in_specs=[pl.BlockSpec(memory_space=pltpu.SMEM)] + whole(len(args) - 1),
        out_specs=jax.tree.map(lambda _: whole(1)[0], out_shape),
        scratch_shapes=[
            pltpu.VMEM((DEPTH * WIDE, CELLS), BF16),
            pltpu.VMEM((2, K, CELLS), BF16),
            pltpu.VMEM((SRC * TAPS, 4, 8, 3 * WIDE), F32),
        ],
        compiler_params=params(),
        cost_estimate=COST,
        name="filter_sums",
    )(*args)


def both_cores(near, far):
    return from_ahead(jnp.stack([near, far]), "core", 1)


def blocks_of(near, far):
    return near, from_ahead(near, "core", 1), far, from_ahead(far, "core", 1)


def blocks_of2(own, core, far):
    return own, from_ahead(core, "core", 1), far, from_ahead(far, "core", 1)


def moved_ahead(blocks, axis):
    return [blocks[0]] + [from_ahead(blocks[d], axis, -d) for d in range(1, 4)]


def total_of(blocks):
    return sum(block.astype(F32) for block in blocks)


def halo(last, first):
    low = lax.ppermute(last, GZ, [(i, i + 1) for i in range(7)])
    high = lax.ppermute(first, GZ, [(i + 1, i) for i in range(7)])
    return low, high


def sum_gz(place, blocks, second):
    part = shape((2, SRC * TAPS * 4, 3 * WIDE))
    mine, other = pl.pallas_call(
        z_sum_kernel,
        out_shape=(part, part),
        in_specs=[pl.BlockSpec(memory_space=pltpu.SMEM)] + whole(5),
        out_specs=tuple(whole(2)),
        compiler_params=params(),
        cost_estimate=COST,
        name="z_sum",
    )(place, *blocks, second)
    return total_of([mine, from_ahead(other, "yl", 1)]).astype(BF16)


def place_filters_kernel(factor_ref, order_ref, own_ref, far_ref, got_ref, first_ref, second_ref):
    orders = [order_ref[src * WIDE : (src + 1) * WIDE, :] for src in range(SRC)]
    for index, out_ref in enumerate((first_ref, second_ref)):
        for kz in range(3):
            lanes = slice(kz * WIDE, (kz + 1) * WIDE)
            total = None
            for order, rows in zip(
                orders,
                (own_ref[index, :, lanes], got_ref[0, index, :, lanes], far_ref[index, :, lanes], got_ref[1, index, :, lanes]),
            ):
                part = lax.dot_general(rows, order, NN, preferred_element_type=F32)
                total = part if total is None else total + part
            total = total * factor_ref[0]
            for tap in range(TAPS):
                out_ref[kz * TAPS + tap] = total[tap * 4 : (tap + 1) * 4]


def near_and_far(sums):
    rows = sums.reshape(2, 2, 2, TAPS * 4, 3 * WIDE).transpose(1, 2, 0, 3, 4)
    return rows, from_ahead(rows[1], "yh", 1)


def finish_filters(order, rows, far, factor):
    got = both_cores(rows[0, 1], far[1])
    outs = pl.pallas_call(
        place_filters_kernel,
        out_shape=(shape((27, 4, 512), F32),) * 2,
        in_specs=[pl.BlockSpec(memory_space=pltpu.SMEM)] + whole(4),
        out_specs=tuple(whole(2)),
        compiler_params=params(),
        cost_estimate=COST,
        name="place_filters",
    )(factor.reshape(1), order, rows[0, 0], far[0], got)
    return [out.reshape(3, 3, 3, 4, 512) for out in outs]


def place_kernel(place_ref, order_ref, own_ref, far_ref, got_ref, out_ref):
    upper = place_ref[2] == 1
    blocks = own_ref, got_ref.at[0], far_ref, got_ref.at[1]
    for pair in range(DEPTH // 2):
        halves = []
        for plane in (2 * pair, 2 * pair + 1):
            rows = jnp.concatenate([ref[plane] for ref in blocks], axis=0)
            halves.append(jnp.where(upper, rows[:, 64:], rows[:, :64]))
        cells = jnp.concatenate(halves, axis=1).T
        part = lax.dot_general(cells, order_ref[...], NN, preferred_element_type=F32).astype(BF16)
        out_ref[2 * pair], out_ref[2 * pair + 1] = part[:64], part[64:]


def finish_image(part, place, order, done):
    near = part[0]
    far = after(from_ahead(part[1], "yh", 1), done)
    out = pl.pallas_call(
        place_kernel,
        out_shape=shape((DEPTH, 64, 512)),
        in_specs=[pl.BlockSpec(memory_space=pltpu.SMEM)] + whole(4),
        out_specs=whole(1)[0],
        compiler_params=params(),
        cost_estimate=COST,
        name="place",
    )(place, order, near, far, both_cores(near, far))
    return out.reshape(DEPTH, 2, ROW, 512)


def after(value, *done):
    return lax.optimization_barrier((value,) + done)[0]


def body(inputs, preact, cotangent, weight1, weight2):
    place = jnp.stack([lax.axis_index(a) for a in AF + GZ]).astype(jnp.int32)
    factor = 1.0 / jnp.sqrt(F32(32 * CELLS))
    planes_first = lambda value: value.transpose(1, 0, 2)
    zero = jnp.zeros((), BF16)
    gather_inputs = lambda value: [value] + [from_ahead(value, "x", d) for d in (1, 2, 3)]

    order = make_orders(place)
    pre = planes_first(preact)
    source = jnp.concatenate([jnp.maximum(pre, zero), planes_first(inputs)])
    ahead, behind = from_ahead(source, "x", 1), from_ahead(source, "x", 3)
    cot = planes_first(cotangent)
    far_cot = from_ahead(cot, "yh", 1)
    low, high = halo(cot[DEPTH - 1 :], cot[:1])
    rims = jnp.concatenate([low, high])
    sources = source, ahead, from_ahead(after(source, far_cot), "x", 2), behind
    own2, core2, far2 = regroup(weight2, order)
    far2 = from_ahead(after(far2, low, high), "yh", 1)
    far_rims = from_ahead(rims, "yh", 1)
    own1, core1, far1 = regroup(weight1, after(order, low))
    far2, far_cot = after((far2, far_cot), far_rims, ahead, behind, own1)
    grads2 = blocks_of(cot, far_cot) + blocks_of(rims, far_rims)
    weights2 = blocks_of2(own2, core2, far2)

    unit_parts = data_by_channel(grads2, after(weights2, *sources))
    far1 = from_ahead(after(far1, unit_parts[0]), "yh", 1)
    one = shape((2, SRC * TAPS * 4, 3 * WIDE))
    every = shape((4,) + one.shape)
    filter2_parts = filter_sums(second_filter_kernel, every, after(place, unit_parts[0]), *grads2, *sources)
    blocks = after(moved_ahead(unit_parts, "x"), filter2_parts)
    grad = jnp.where(pre > 0, total_of(blocks), 0.0).astype(BF16)
    grad = after(grad, far1)
    low, high = halo(grad[DEPTH - 1 :], grad[:1])
    far_grad = from_ahead(grad, "yh", 1)
    rims = jnp.concatenate([low, high])
    far_rims = from_ahead(rims, "yh", 1)
    filter2_got = lax.all_to_all(filter2_parts, "z", 0, 0)
    weights1 = blocks_of2(own1, core1, after(far1, low))
    grads1 = blocks_of(grad, far_grad) + blocks_of(rims, far_rims)
    *filter_parts, filter2_sum = filter_sums(
        first_filter_kernel, (one,) * 5, place, *grads1, *sources, filter2_got
    )
    image_parts = data_by_row(after(place, filter_parts[0]), grads1, weights1)
    filter1_got = after(moved_ahead(filter_parts, "z"), image_parts[0])
    sums = sum_gz(place, filter1_got, filter2_sum)
    rows, far = near_and_far(sums)
    blocks = after(moved_ahead(image_parts, "x"), far)
    filter1_grad, filter2_grad = finish_filters(order, rows, far, factor)
    input_grad = finish_image(total_of(blocks).astype(BF16), place, order, filter1_grad)
    return input_grad, filter1_grad, filter2_grad


def solution(mesh):
    fine = Mesh(mesh.devices.reshape(2, 4, 2, 4, 2), AF + GZ)
    placed = (
        P(AF, GZ, None),
        P(AF, GZ, None),
        P(AF, GZ, None),
        P(None, None, None, AF, None),
        P(None, None, None, AF, None),
    )
    return jax.shard_map(
        body,
        mesh=fine,
        in_specs=placed,
        out_specs=(
            P(GZ, AF, None, None),
            P(None, None, None, AF + GZ, None),
            P(None, None, None, AF + GZ, None),
        ),
        check_vma=False,
    )
```
